256 devices in a mesh: tile: 32 (over x, z_hi, core), tracer: 8 (over y, z_lo).
Axes of the slice: x: 4, y: 4, z: 8 (z_hi: 4, z_lo: 2; z = z_hi * 2 + z_lo), core: 2. Of those that a mesh axis runs over, the one named last changes fastest.
Arguments:
- tracers: float32 [16, 32, 8, 128, 128], P('tracer', 'tile'), may hold values from -16 to 16
- east_velocity: bfloat16 [32, 8, 128, 128], P('tile', 'tracer'), may hold values from -0.5 to 0.5
- north_velocity: bfloat16 [32, 8, 128, 128], P('tile', 'tracer'), may hold values from -0.5 to 0.5
- diffusivity: bfloat16 [32, 8], P('tile', 'tracer'), may hold values from 0.0099487305 to 0.14941406
- vertical_diffusivity: float32 [8], replicated, may hold values from 0.02 to 0.2
- depths: int32 [32], replicated, may hold values from 1 to 8
- neighbours: int32 [32, 4], replicated, may hold values from -1 to 31, as said below
Outputs:
- transported: float32 [16, 32, 8, 128, 128], P('tracer', 'tile')
The draws below stay inside these ranges and needn't reach their ends.
Inputs may be any that keep to these rules, and one draw needn't show every extreme that they name: `neighbours`: tiles are the wet places of a face of 2 x 24 tile places, numbered row by row. Entry [s, e] is the slot of the wet tile beside slot s to the west, east, south or north (e = 0, 1, 2, 3), or -1 where that place is land or off the strip. The relation is symmetric; a west or east neighbour of slot s is s - 1 or s + 1, and a south or north neighbour lies at most 2 slots below or above s. The first 10 rows of places and the last 3 places hold no land.
All inputs are finite; a program needn't handle non-finite values.
Results may differ from the reference program's by a relative error of at most 0.0003.
Values may be sent and summed in bfloat16 or wider, within the bound.
No kernel may reach another device: no remote copies, remote signals or barrier semaphores. Data moves between devices by JAX's collectives and lax.ppermute only.
A program may use at most 64 MiB of HBM per device.

```python
import math
import jax
import jax.numpy as jnp
from jax import lax

S = 128
K = 8
TILES = 32
TRACERS = 16
GRID_COLUMNS = 2
GRID_ROWS = 24
WET_ROWS = 10


def draw_neighbours(key, part):
    key = jax.random.fold_in(key, 7)
    places = GRID_COLUMNS * GRID_ROWS
    prefix = WET_ROWS * GRID_COLUMNS
    tail = GRID_COLUMNS + 1
    spare = places - prefix - tail
    land_count = places - TILES
    order = jax.random.permutation(key, spare)
    middle_wet = order >= land_count
    is_wet = jnp.concatenate([jnp.ones((prefix,), bool), middle_wet, jnp.ones((tail,), bool)])
    slot = jnp.cumsum(is_wet.astype(jnp.int32)) - 1
    place = jnp.arange(places, dtype=jnp.int32)
    column = place % GRID_COLUMNS

    def look(target, inside):
        safe = jnp.clip(target, 0, places - 1)
        usable = inside & (target >= 0) & (target < places) & is_wet[safe]
        return jnp.where(usable, slot[safe], -1)
    west = look(place - 1, column > 0)
    east = look(place + 1, column < GRID_COLUMNS - 1)
    south = look(place - GRID_COLUMNS, place >= GRID_COLUMNS)
    north = look(place + GRID_COLUMNS, place < places - GRID_COLUMNS)
    table = jnp.stack([west, east, south, north], 1).astype(jnp.int32)
    index = jnp.where(is_wet, slot, TILES)
    result = jnp.zeros((TILES, 4), jnp.int32).at[index].set(table, mode='drop')
    return result.astype(jnp.int32)


def draw_tracers(key, part):
    key = jax.random.fold_in(key, 11)
    shape = (TRACERS, TILES, K, S, S)
    cell = jnp.arange(S, dtype=jnp.int32)
    outer = jnp.minimum(cell, S - 1 - cell) < 3
    band = outer[:, None] | outer[None, :]
    factor = jnp.where(band, 4.0, 1.0).astype(jnp.float32)
    base = jnp.clip(jax.random.normal(key, shape, jnp.float32), -4.0, 4.0)
    return (base * factor).astype(jnp.float32)


def set_ends(values, rng, low, high):
    shape = values.shape
    spot = [jax.random.randint(jax.random.fold_in(rng, axis), (), 0, shape[axis]) for axis in range(len(shape))]
    values = values.at[tuple(spot)].set(low)
    longest = shape.index(max(shape))
    spot[longest] = (spot[longest] + 1) % shape[longest]
    return values.at[tuple(spot)].set(high)


def steps_of(stream_key, dims, shards, low, high):
    def one(position, blocks):
        heights = jax.random.uniform(jax.random.fold_in(jax.random.fold_in(stream_key, 6), position), (blocks,), jnp.float32, low / len(shards), high / len(shards))
        return jnp.repeat(jnp.exp(heights), dims[position] // blocks).reshape((-1,) + (1,) * (len(dims) - position - 1))

    gain = one(*shards[0])
    for cut in shards[1:]:
        gain = gain * one(*cut)
    return gain


def setup_inputs(seed: int = 0) -> dict:
    splits = jax.random.split(jax.random.key(seed), 8)
    return {
        "tracers": draw_tracers(jax.random.fold_in(splits[7], 71), 0),
        "east_velocity": jnp.clip(jax.random.uniform(splits[1], (TILES, K, S, S), jnp.float32, -0.5, 0.5) * steps_of(splits[1], (TILES, K, S, S), ((0, 32), (1, 8)), -0.4, 0.0), -0.5, 0.5).astype(jnp.bfloat16),
        "north_velocity": jnp.clip(jax.random.uniform(splits[2], (TILES, K, S, S), jnp.float32, -0.5, 0.5) * steps_of(splits[2], (TILES, K, S, S), ((0, 32), (1, 8)), -0.4, 0.0), -0.5, 0.5).astype(jnp.bfloat16),
        "diffusivity": jnp.clip(jnp.exp(math.log(0.14941406) - 2.7092764 * jax.random.uniform(splits[3], (TILES, K), jnp.float32) ** steps_of(splits[3], (TILES, K), ((0, 32), (1, 8)), -0.2, 0.2)), 0.0099487305, 0.14941406).astype(jnp.bfloat16),
        "vertical_diffusivity": jnp.clip(jnp.exp(jax.random.uniform(splits[4], (K,), jnp.float32, math.log(0.02), math.log(0.2))), 0.02, 0.2),
        "depths": set_ends(jax.random.randint(splits[5], (TILES,), 1, K + 1), jax.random.fold_in(splits[5], 1), 1, K).astype(jnp.int32),
        "neighbours": draw_neighbours(jax.random.fold_in(splits[7], 71), 0),
    }


def shifted(values, lower_ghost, upper_ghost, offset, axis):
    extent = values.shape[axis]
    if offset == 0:
        return values
    if offset > 0:
        return jnp.concatenate([lax.slice_in_dim(values, offset, extent, axis=axis), lax.slice_in_dim(upper_ghost, 0, offset, axis=axis)], axis)
    return jnp.concatenate([lax.slice_in_dim(lower_ghost, 3 + offset, 3, axis=axis), lax.slice_in_dim(values, 0, extent + offset, axis=axis)], axis)


def direction_terms(values, lower_ghost, upper_ghost, velocity, axis):
    samples = [shifted(values, lower_ghost, upper_ghost, offset, axis) for offset in range(-3, 4)]
    ahead = (-2.0 * samples[0] + 15.0 * samples[1] - 60.0 * samples[2] + 20.0 * samples[3] + 30.0 * samples[4] - 3.0 * samples[5]) / 60.0
    behind = (3.0 * samples[1] - 30.0 * samples[2] - 20.0 * samples[3] + 60.0 * samples[4] - 15.0 * samples[5] + 2.0 * samples[6]) / 60.0
    slope = jnp.where(velocity >= 0, ahead, behind)
    return velocity * slope, samples[2] + samples[4] - 2.0 * samples[3]


def tendency(values, west_ghost, east_ghost, south_ghost, north_ghost, east_flow, north_flow, mixing, vertical, wet):
    x_axis = values.ndim - 1
    y_axis = values.ndim - 2
    z_axis = values.ndim - 3
    levels = values.shape[z_axis]
    carry_x, curve_x = direction_terms(values, west_ghost, east_ghost, east_flow, x_axis)
    carry_y, curve_y = direction_terms(values, south_ghost, north_ghost, north_flow, y_axis)
    zero_level = jnp.zeros_like(lax.slice_in_dim(values, 0, 1, axis=z_axis))
    above = jnp.concatenate([lax.slice_in_dim(values, 1, levels, axis=z_axis), zero_level], z_axis)
    below = jnp.concatenate([zero_level, lax.slice_in_dim(values, 0, levels - 1, axis=z_axis)], z_axis)
    return wet * (mixing * (curve_x + curve_y) - carry_x - carry_y + vertical * (above + below - 2.0 * values))


def neighbour_ghosts(values, neighbours):
    count = values.shape[0]
    extent = values.shape[-1]
    safe = jnp.clip(neighbours, 0, count - 1).astype(jnp.int32)
    present = neighbours >= 0

    def pick(strip, side):
        taken = jnp.take(strip, safe[:, side], axis=0)
        return jnp.where(present[:, side][:, None, None, None], taken, jnp.zeros_like(taken))

    west_ghost = pick(values[:, :, :, extent - 3:], 0)
    east_ghost = pick(values[:, :, :, :3], 1)
    south_ghost = pick(values[:, :, extent - 3:, :], 2)
    north_ghost = pick(values[:, :, :3, :], 3)
    return west_ghost, east_ghost, south_ghost, north_ghost


def reference(tracers, east_velocity, north_velocity, diffusivity, vertical_diffusivity, depths, neighbours):
    levels = tracers.shape[2]
    wet = (jnp.arange(levels)[None, :] < depths[:, None]).astype(jnp.float32)[:, :, None, None]
    east_flow = east_velocity.astype(jnp.float32)
    north_flow = north_velocity.astype(jnp.float32)
    mixing = diffusivity.astype(jnp.float32)[:, :, None, None]
    vertical = vertical_diffusivity[:, None, None]

    def advance(values):
        west_ghost, east_ghost, south_ghost, north_ghost = neighbour_ghosts(values, neighbours)
        return tendency(values, west_ghost, east_ghost, south_ghost, north_ghost, east_flow, north_flow, mixing, vertical, wet)

    def single(field_in):
        start = field_in * wet
        section = start + advance(start)
        return 0.5 * (start + section + advance(section))

    return lax.map(single, tracers)
```

```python
import functools

import jax
import jax.numpy as jnp
from jax import lax
from jax.experimental import pallas as pl
from jax.experimental.pallas import tpu as pltpu
from jax.sharding import PartitionSpec as P

S = 128
LEVELS = 8
TILES = 32
AHEAD = (-2.0, 15.0, -60.0, 20.0, 30.0, -3.0, 0.0)
BEHIND = (0.0, 3.0, -30.0, -20.0, 60.0, -15.0, 2.0)
CURVE = (0.0, 0.0, 1.0, -2.0, 1.0, 0.0, 0.0)
BANDS = (AHEAD, BEHIND, CURVE)

ROUNDS = (
    [(s, s ^ 2) for s in range(TILES)],
    [(s, ((s - 2) ^ 2) + 2) for s in range(2, TILES - 2)],
    [(s, s ^ 1) for s in range(TILES)],
    [(s, s + 1 if s % 2 else s - 1) for s in range(19, 29)],
)


def partners(tile):
    middle = (tile >= 19) & (tile < 29)
    odd = jnp.where(tile % 2 == 1, tile + 1, tile - 1)
    return (
        jnp.where((tile // 2) % 2 == 0, tile + 2, tile - 2),
        jnp.where((tile // 2) % 2 == 1, tile + 2, tile - 2),
        jnp.where(tile % 2 == 0, tile + 1, tile - 1),
        jnp.where(middle, odd, -9),
    )


def band(distance, coefficients):
    total = jnp.zeros(distance.shape, jnp.float32)
    for step, coefficient in zip(range(-3, 4), coefficients):
        if coefficient:
            total = jnp.where(distance == step, coefficient, total)
    return total


def iota(shape, dim):
    return lax.broadcasted_iota(jnp.int32, shape, dim)


def bands_right(source, width):
    out = iota((width, S), 1)
    return jnp.concatenate([band(source - out, c) for c in BANDS], 1).astype(jnp.bfloat16)


def bands_left(source, width):
    out = iota((S, width), 0)
    return jnp.concatenate([band(source - out, c) for c in BANDS], 0).astype(jnp.bfloat16)


def rims(read, side_east, near, tile, out_refs):
    lane_block = iota((S, S), 1) // 8
    shift = jnp.where(side_east, 8, 0)
    x_rim = jnp.zeros((S, S), jnp.float32)
    for p in range(2 * LEVELS):
        plane = read(p)
        x_rim = jnp.where(lane_block == p, pltpu.roll(plane, shift + 8 * p, 1), x_rim)
    south = jnp.concatenate([read(p)[:8] for p in range(2 * LEVELS)], 0)
    north = jnp.concatenate([read(p)[S - 8 :] for p in range(2 * LEVELS)], 0)
    for slot, ref in zip(partners(tile), out_refs):
        is_x = ((slot == near[0]) | (slot == near[1])).astype(jnp.float32)
        is_n = (slot == near[3]).astype(jnp.float32)
        y_rim = jnp.where(is_n > 0, north, south)
        ref[...] = jnp.where(is_x > 0, x_rim, y_rim).astype(jnp.bfloat16)


def first_kernel(tracers, east, north, mixing, depths, neighbours, flow_out, *rim_refs):
    tile = lax.axis_index("tile")
    near = [neighbours[tile, e] for e in range(4)]
    depth = depths[tile]
    block = jnp.concatenate(
        [
            east[...],
            north[...],
            jnp.broadcast_to(mixing[...].astype(jnp.float32), (16, S)).astype(jnp.bfloat16),
        ],
        0,
    )
    for j in range(LEVELS):
        flow_out[j] = block

    def read(p):
        return tracers[p] * (p % LEVELS < depth).astype(jnp.float32)

    rims(read, near[1] >= 0, near, tile, rim_refs)


def substep(values, flow, near, tile, received, vertical, depth, emit):
    planes = 2 * LEVELS
    gx = jnp.zeros((S, S), jnp.float32)
    gs = jnp.zeros((S, S), jnp.float32)
    gn = jnp.zeros((S, S), jnp.float32)
    for slot, ref in zip(partners(tile), received):
        block = ref[...].astype(jnp.float32)
        gx = jnp.where((slot == near[0]) | (slot == near[1]), block, gx)
        gs = jnp.where(slot == near[2], block, gs)
        gn = jnp.where(slot == near[3], block, gn)
    base = jnp.where(near[1] >= 0, S, -8)
    own_right = bands_right(iota((S, S), 0), S)
    right = jnp.concatenate([own_right, own_right], 0)
    ghost_right = bands_right(iota((S, S), 0) % 8 + base, S)
    own_left = bands_left(iota((S, S), 1), S)
    left = jnp.concatenate([own_left, own_left], 1)
    column = iota((S, 16), 1)
    ghost_left = bands_left(jnp.where(column < 8, column - 8, column + S - 8), 16)
    lane_block = iota((S, S), 1) // 8

    def dot(a, b):
        return jnp.dot(a, b, preferred_element_type=jnp.float32)

    for k in range(LEVELS):
        pair = [values(k), values(k + LEVELS)]
        high = [q.astype(jnp.bfloat16) for q in pair]
        low = [(q - h.astype(jnp.float32)).astype(jnp.bfloat16) for q, h in zip(pair, high)]
        rows = jnp.concatenate(
            [jnp.concatenate([h, l], 1) for h, l in zip(high, low)], 0
        )
        ghosts = jnp.concatenate(
            [jnp.where(lane_block == p, gx, 0.0).astype(jnp.bfloat16) for p in (k, k + LEVELS)], 0
        )
        along_x = dot(rows, right) + dot(ghosts, ghost_right)
        columns = jnp.concatenate(
            [jnp.concatenate([h, l], 0) for h, l in zip(high, low)], 1
        )
        edge = jnp.concatenate(
            [
                jnp.concatenate([gs[8 * p : 8 * p + 8], gn[8 * p : 8 * p + 8]], 0)
                for p in (k, k + LEVELS)
            ],
            1,
        ).astype(jnp.bfloat16)
        along_y = dot(left, columns) + dot(ghost_left, edge)
        u = flow[k, :S].astype(jnp.float32)
        v = flow[k, S : 2 * S].astype(jnp.float32)
        mixing = flow[k, 2 * S : 2 * S + 16].astype(jnp.float32)[:1]
        wet = (k < depth).astype(jnp.float32)
        lift = vertical[k]
        for t in range(2):
            x = along_x[t * S : (t + 1) * S]
            y = along_y[:, t * S : (t + 1) * S]
            q = pair[t]
            slope_x = jnp.where(u >= 0, x[:, :S], x[:, S : 2 * S])
            slope_y = jnp.where(v >= 0, y[:S], y[S : 2 * S])
            carry = (u * slope_x + v * slope_y) * (1.0 / 60.0)
            curve = x[:, 2 * S :] + y[2 * S :]
            column_sum = -2.0 * q
            if k > 0:
                column_sum = column_sum + values(k - 1 + t * LEVELS)
            if k < LEVELS - 1:
                column_sum = column_sum + values(k + 1 + t * LEVELS)
            emit(k + t * LEVELS, wet * (mixing * curve - carry + lift * column_sum))


def second_kernel(
    tracers, flow, vertical, depths, neighbours, a, b, c, d, section, *rim_refs
):
    tile = lax.axis_index("tile")
    near = [neighbours[tile, e] for e in range(4)]
    depth = depths[tile]

    def start(p):
        return tracers[p] * (p % LEVELS < depth).astype(jnp.float32)

    def emit(p, change):
        section[p] = start(p) + change

    substep(start, flow, near, tile, (a, b, c, d), vertical, depth, emit)
    rims(lambda p: section[p], near[1] >= 0, near, tile, rim_refs)


def third_kernel(
    tracers, section, flow, vertical, depths, neighbours, a, b, c, d, out
):
    tile = lax.axis_index("tile")
    near = [neighbours[tile, e] for e in range(4)]
    depth = depths[tile]

    def emit(p, change):
        start = tracers[p] * (p % LEVELS < depth).astype(jnp.float32)
        out[p] = 0.5 * (start + section[p] + change)

    substep(lambda p: section[p], flow, near, tile, (a, b, c, d), vertical, depth, emit)


VMEM = pl.BlockSpec(memory_space=pltpu.VMEM)
SMEM = pl.BlockSpec(memory_space=pltpu.SMEM)
PARAMS = pltpu.CompilerParams(vmem_limit_bytes=48 * 1024 * 1024)
RIM = jax.ShapeDtypeStruct((S, S), jnp.bfloat16)


def swap(blocks):
    return [lax.ppermute(x, "tile", pairs) for x, pairs in zip(blocks, ROUNDS)]


def local(
    tracers, east_velocity, north_velocity, diffusivity, vertical_diffusivity, depths, neighbours
):
    planes = 2 * LEVELS
    field = tracers.reshape(planes, S, S)
    flow, *blocks = pl.pallas_call(
        first_kernel,
        out_shape=[jax.ShapeDtypeStruct((LEVELS, 2 * S + 16, S), jnp.bfloat16)] + [RIM] * 4,
        in_specs=[VMEM] * 4 + [SMEM] * 2,
        out_specs=[VMEM] * 5,
        compiler_params=PARAMS,
        name="rims",
    )(
        field,
        east_velocity.reshape(S, S),
        north_velocity.reshape(S, S),
        diffusivity,
        depths,
        neighbours,
    )
    flow = lax.all_to_all(flow, "tracer", 0, 0)
    section, *blocks = pl.pallas_call(
        second_kernel,
        out_shape=[jax.ShapeDtypeStruct((planes, S, S), jnp.float32)] + [RIM] * 4,
        in_specs=[VMEM] * 2 + [SMEM] * 3 + [VMEM] * 4,
        out_specs=[VMEM] * 5,
        compiler_params=PARAMS,
        name="section",
    )(field, flow, vertical_diffusivity, depths, neighbours, *swap(blocks))
    out = pl.pallas_call(
        third_kernel,
        out_shape=jax.ShapeDtypeStruct((planes, S, S), jnp.float32),
        in_specs=[VMEM] * 3 + [SMEM] * 3 + [VMEM] * 4,
        out_specs=VMEM,
        compiler_params=PARAMS,
        name="transported",
    )(field, section, flow, vertical_diffusivity, depths, neighbours, *swap(blocks))
    return out.reshape(tracers.shape)


def solution(mesh):
    return jax.shard_map(
        local,
        mesh=mesh,
        in_specs=(
            P("tracer", "tile", None, None, None),
            P("tile", "tracer", None, None),
            P("tile", "tracer", None, None),
            P("tile", "tracer"),
            P(),
            P(),
            P(),
        ),
        out_specs=P("tracer", "tile", None, None, None),
        check_vma=False,
    )
```

```python
import jax
import jax.numpy as jnp
from jax import lax
from jax.experimental import pallas as pl
from jax.experimental.pallas import tpu as pltpu
from jax.sharding import PartitionSpec as P

S = 128
LEVELS = 8
TILES = 32
AHEAD = (-2.0, 15.0, -60.0, 20.0, 30.0, -3.0, 0.0)
BEHIND = (0.0, 3.0, -30.0, -20.0, 60.0, -15.0, 2.0)
CURVE = (0.0, 0.0, 1.0, -2.0, 1.0, 0.0, 0.0)
BANDS = (AHEAD, BEHIND, CURVE)

MATES = [(s, s ^ 1) for s in range(TILES)]
ACROSS = [(s, s + 3) for s in range(0, TILES - 3, 2)] + [(s + 3, s) for s in range(0, TILES - 3, 2)]


def beside(neighbours, tile):
    row = [neighbours[tile, e] for e in range(4)]
    return [jnp.where(slot < 0, -9, slot) for slot in row]


def band(distance, coefficients):
    total = jnp.zeros(distance.shape, jnp.float32)
    for step, coefficient in zip(range(-3, 4), coefficients):
        if coefficient:
            total = jnp.where(distance == step, coefficient, total)
    return total


def iota(shape, dim):
    return lax.broadcasted_iota(jnp.int32, shape, dim)


def bands_right(source, width):
    out = iota((width, S), 1)
    return jnp.concatenate([band(source - out, c) for c in BANDS], 1).astype(jnp.bfloat16)


def bands_left(source, width):
    out = iota((S, width), 0)
    return jnp.concatenate([band(source - out, c) for c in BANDS], 0).astype(jnp.bfloat16)


def rims(read, side_east, tile, out):
    planes = 2 * LEVELS
    lane = iota((S, S), 1)
    shift = jnp.where(side_east, 4, 0)
    x_rim = jnp.zeros((S, S), jnp.float32)
    for p in range(planes):
        x_rim = jnp.where(lane // 4 == p, pltpu.roll(read(p), shift + 4 * p, 1), x_rim)
    half = S // 2
    x_rim = jnp.where(lane[:half] < half, x_rim[:half], pltpu.roll(x_rim[half:], half, 1))
    low = iota((8, S), 0) < 4
    south, north = [], []
    for p in range(0, planes, 2):
        first, second = read(p), read(p + 1)
        south.append(jnp.where(low, first[:8], pltpu.roll(second[:8], 4, 0)))
        north.append(jnp.where(low, pltpu.roll(first[S - 8 :], 4, 0), second[S - 8 :]))
    south, north = jnp.concatenate(south, 0), jnp.concatenate(north, 0)
    even = tile % 2 == 0
    out[0] = x_rim.astype(jnp.bfloat16)
    out[1] = jnp.where(even, south, north).astype(jnp.bfloat16)
    out[2] = jnp.where(even, north, south).astype(jnp.bfloat16)


def first_kernel(
    tracers_in,
    east_in,
    north_in,
    mixing_in,
    depths_in,
    neighbours_in,
    flow_out,
    rims_out,
    tracers,
    east,
    north,
    mixing,
    depths,
    neighbours,
    arrived,
):
    copies = [
        pltpu.make_async_copy(source, target, arrived.at[i])
        for i, (source, target) in enumerate(
            (
                (east_in, east),
                (north_in, north),
                (mixing_in, mixing),
                (depths_in, depths),
                (neighbours_in, neighbours),
                (tracers_in, tracers),
            )
        )
    ]
    for copy in copies:
        copy.start()
    for copy in copies[:3]:
        copy.wait()
    block = jnp.concatenate(
        [
            east[...],
            north[...],
            jnp.broadcast_to(mixing[...].astype(jnp.float32), (16, S)).astype(jnp.bfloat16),
        ],
        0,
    )
    for j in range(LEVELS):
        flow_out[j] = block
    for copy in copies[3:]:
        copy.wait()
    tile = lax.axis_index("tile")
    depth = depths[tile]

    def read(p):
        return tracers[p] * (p % LEVELS < depth).astype(jnp.float32)

    rims(read, neighbours[tile, 1] >= 0, tile, rims_out)


def substep(values, flow, near, tile, received, vertical, depth, emit):
    planes = 2 * LEVELS
    gx = jnp.zeros((S // 2, S), jnp.float32)
    gs = jnp.zeros((S // 2, S), jnp.float32)
    gn = jnp.zeros((S // 2, S), jnp.float32)
    mate, own, other = received
    toward = jnp.where(tile % 2 == 0, 1, -1)
    for steps, x_block, y_block in (
        (1, mate.at[0], mate.at[2]),
        (2, None, own.at[1]),
        (-1, other.at[0], other.at[1]),
        (-2, None, other.at[2]),
    ):
        slot = tile + steps * toward
        if x_block is not None:
            in_row = (slot == near[0]) | (slot == near[1])
            gx = jnp.where(in_row, x_block[...].astype(jnp.float32), gx)
        block = y_block[...].astype(jnp.float32)
        gs = jnp.where(slot == near[2], block, gs)
        gn = jnp.where(slot == near[3], block, gn)
    gx = jnp.concatenate([gx, pltpu.roll(gx, S // 2, 1)], 0)
    base = jnp.where(near[1] >= 0, S, -4)
    own_right = bands_right(iota((S, S), 0), S)
    right = jnp.concatenate([own_right, own_right], 0)
    ghost_right = bands_right(iota((S, S), 0) % 4 + base, S)
    own_left = bands_left(iota((S, S), 1), S)
    left = jnp.concatenate([own_left, own_left], 1)
    column = iota((S, 16), 1)
    source = jnp.where(column < 8, column % 4 - 4, column % 4 + S)
    ghost_left = [
        bands_left(jnp.where((column // 4) % 2 == odd, source, -2 * S), 16) for odd in range(2)
    ]
    lane_block = iota((S, S), 1) // 4

    def dot(a, b):
        return jnp.dot(a, b, preferred_element_type=jnp.float32)

    for k in range(LEVELS):
        pair = [values(k), values(k + LEVELS)]
        high = [q.astype(jnp.bfloat16) for q in pair]
        low = [(q - h.astype(jnp.float32)).astype(jnp.bfloat16) for q, h in zip(pair, high)]
        rows = jnp.concatenate(
            [jnp.concatenate([h, l], 1) for h, l in zip(high, low)], 0
        )
        ghosts = jnp.concatenate(
            [jnp.where(lane_block == p, gx, 0.0).astype(jnp.bfloat16) for p in (k, k + LEVELS)], 0
        )
        along_x = dot(rows, right) + dot(ghosts, ghost_right)
        columns = jnp.concatenate(
            [jnp.concatenate([h, l], 0) for h, l in zip(high, low)], 1
        )
        edge = jnp.concatenate(
            [
                jnp.concatenate([gs[8 * t : 8 * t + 8], gn[8 * t : 8 * t + 8]], 0)
                for t in (k // 2, (k + LEVELS) // 2)
            ],
            1,
        ).astype(jnp.bfloat16)
        along_y = dot(left, columns) + dot(ghost_left[k % 2], edge)
        u = flow[k, :S].astype(jnp.float32)
        v = flow[k, S : 2 * S].astype(jnp.float32)
        mixing = flow[k, 2 * S : 2 * S + 16].astype(jnp.float32)[:1]
        wet = (k < depth).astype(jnp.float32)
        lift = vertical[k]
        for t in range(2):
            x = along_x[t * S : (t + 1) * S]
            y = along_y[:, t * S : (t + 1) * S]
            q = pair[t]
            slope_x = jnp.where(u >= 0, x[:, :S], x[:, S : 2 * S])
            slope_y = jnp.where(v >= 0, y[:S], y[S : 2 * S])
            carry = (u * slope_x + v * slope_y) * (1.0 / 60.0)
            curve = x[:, 2 * S :] + y[2 * S :]
            column_sum = -2.0 * q
            if k > 0:
                column_sum = column_sum + values(k - 1 + t * LEVELS)
            if k < LEVELS - 1:
                column_sum = column_sum + values(k + 1 + t * LEVELS)
            emit(k + t * LEVELS, wet * (mixing * curve - carry + lift * column_sum))


def second_kernel(
    tracers, flow, vertical, depths, neighbours, mate, own, other, section, rims_out
):
    tile = lax.axis_index("tile")
    near = beside(neighbours, tile)
    depth = depths[tile]

    def start(p):
        return tracers[p] * (p % LEVELS < depth).astype(jnp.float32)

    def emit(p, change):
        section[p] = start(p) + change

    substep(start, flow, near, tile, (mate, own, other), vertical, depth, emit)
    rims(lambda p: section[p], near[1] >= 0, tile, rims_out)


def third_kernel(
    tracers, section, flow, vertical, depths, neighbours, mate, own, other, out
):
    tile = lax.axis_index("tile")
    near = beside(neighbours, tile)
    depth = depths[tile]

    def emit(p, change):
        start = tracers[p] * (p % LEVELS < depth).astype(jnp.float32)
        out[p] = 0.5 * (start + section[p] + change)

    received = (mate, own, other)
    substep(lambda p: section[p], flow, near, tile, received, vertical, depth, emit)


VMEM = pl.BlockSpec(memory_space=pltpu.VMEM)
SMEM = pl.BlockSpec(memory_space=pltpu.SMEM)
HBM = pl.BlockSpec(memory_space=pltpu.HBM)
PARAMS = pltpu.CompilerParams(vmem_limit_bytes=48 * 1024 * 1024)
RIMS = jax.ShapeDtypeStruct((3, S // 2, S), jnp.bfloat16)


def exchange(blocks):
    mate = lax.ppermute(blocks, "tile", MATES)
    own = lax.ppermute(jnp.concatenate([mate[:2], blocks[2:]], 0), "tile", ACROSS)
    return mate, own, lax.ppermute(own, "tile", MATES)


def local(
    tracers, east_velocity, north_velocity, diffusivity, vertical_diffusivity, depths, neighbours
):
    planes = 2 * LEVELS
    field = tracers.reshape(planes, S, S)
    flow, blocks = pl.pallas_call(
        first_kernel,
        out_shape=[jax.ShapeDtypeStruct((LEVELS, 2 * S + 16, S), jnp.bfloat16), RIMS],
        in_specs=[HBM] * 6,
        out_specs=[VMEM] * 2,
        scratch_shapes=[
            pltpu.VMEM((planes, S, S), jnp.float32),
            pltpu.VMEM((S, S), jnp.bfloat16),
            pltpu.VMEM((S, S), jnp.bfloat16),
            pltpu.VMEM((1, 1), jnp.bfloat16),
            pltpu.SMEM((TILES,), jnp.int32),
            pltpu.SMEM((TILES, 4), jnp.int32),
            pltpu.SemaphoreType.DMA((6,)),
        ],
        compiler_params=pltpu.CompilerParams(vmem_limit_bytes=62 * 1024 * 1024),
        name="rims",
    )(
        field,
        east_velocity.reshape(S, S),
        north_velocity.reshape(S, S),
        diffusivity,
        depths,
        neighbours,
    )
    flow = lax.all_to_all(flow, "tracer", 0, 0)
    section, blocks = pl.pallas_call(
        second_kernel,
        out_shape=[jax.ShapeDtypeStruct((planes, S, S), jnp.float32), RIMS],
        in_specs=[VMEM] * 2 + [SMEM] * 3 + [VMEM] * 3,
        out_specs=[VMEM] * 2,
        compiler_params=PARAMS,
        name="section",
    )(field, flow, vertical_diffusivity, depths, neighbours, *exchange(blocks))
    out = pl.pallas_call(
        third_kernel,
        out_shape=jax.ShapeDtypeStruct((planes, S, S), jnp.float32),
        in_specs=[VMEM] * 3 + [SMEM] * 3 + [VMEM] * 3,
        out_specs=VMEM,
        compiler_params=PARAMS,
        name="transported",
    )(field, section, flow, vertical_diffusivity, depths, neighbours, *exchange(blocks))
    return out.reshape(tracers.shape)


def solution(mesh):
    return jax.shard_map(
        local,
        mesh=mesh,
        in_specs=(
            P("tracer", "tile", None, None, None),
            P("tile", "tracer", None, None),
            P("tile", "tracer", None, None),
            P("tile", "tracer"),
            P(),
            P(),
            P(),
        ),
        out_specs=P("tracer", "tile", None, None, None),
        check_vma=False,
    )
```

```python
import jax
import jax.numpy as jnp
from jax import lax
from jax.experimental import pallas as pl
from jax.experimental.pallas import tpu as pltpu
from jax.sharding import PartitionSpec as P

S = 128
LEVELS = 8
TILES = 32
AHEAD = (-2.0, 15.0, -60.0, 20.0, 30.0, -3.0, 0.0)
BEHIND = (0.0, 3.0, -30.0, -20.0, 60.0, -15.0, 2.0)
CURVE = (0.0, 0.0, 1.0, -2.0, 1.0, 0.0, 0.0)
BANDS = (AHEAD, BEHIND, CURVE)

MATES = [(s, s ^ 1) for s in range(TILES)]
ACROSS = [(s, s + 3) for s in range(0, TILES - 3, 2)] + [(s + 3, s) for s in range(0, TILES - 3, 2)]


def beside(neighbours, tile):
    row = [neighbours[e, tile] for e in range(4)]
    return [jnp.where(slot < 0, -9, slot) for slot in row]


def band(distance, coefficients):
    total = jnp.zeros(distance.shape, jnp.float32)
    for step, coefficient in zip(range(-3, 4), coefficients):
        if coefficient:
            total = jnp.where(distance == step, coefficient, total)
    return total


def iota(shape, dim):
    return lax.broadcasted_iota(jnp.int32, shape, dim)


def bands_right(source, width):
    out = iota((width, S), 1)
    return jnp.concatenate([band(source - out, c) for c in BANDS], 1).astype(jnp.bfloat16)


def bands_left(source, out):
    return jnp.concatenate([band(source - out, c) for c in BANDS], 0).astype(jnp.bfloat16)


def rims(read, side_east, tile, out):
    planes = 2 * LEVELS
    lane = iota((S, S), 1)
    shift = jnp.where(side_east, 4, 0)
    x_rim = jnp.zeros((S, S), jnp.float32)
    for p in range(planes):
        x_rim = jnp.where(lane // 4 == p, pltpu.roll(read(p), shift + 4 * p, 1), x_rim)
    half = S // 2
    x_rim = jnp.where(lane[:half] < half, x_rim[:half], pltpu.roll(x_rim[half:], half, 1))
    low = iota((8, S), 0) < 4
    south, north = [], []
    for p in range(0, planes, 2):
        first, second = read(p), read(p + 1)
        south.append(jnp.where(low, first[:8], pltpu.roll(second[:8], 4, 0)))
        north.append(jnp.where(low, pltpu.roll(first[S - 8 :], 4, 0), second[S - 8 :]))
    south, north = jnp.concatenate(south, 0), jnp.concatenate(north, 0)
    even = tile % 2 == 0
    out[0] = x_rim.astype(jnp.bfloat16)
    out[1] = jnp.where(even, south, north).astype(jnp.bfloat16)
    out[2] = jnp.where(even, north, south).astype(jnp.bfloat16)


def first_kernel(
    tracers_in,
    east_in,
    north_in,
    mixing,
    depths_in,
    neighbours_in,
    vertical_in,
    flow_out,
    rims_out,
    start_out,
    levels_out,
    tracers,
    east,
    north,
    depths,
    neighbours,
    vertical,
    arrived,
):
    copies = [
        pltpu.make_async_copy(source, target, arrived.at[i])
        for i, (source, target) in enumerate(
            (
                (east_in, east),
                (north_in, north),
                (depths_in, depths),
                (neighbours_in, neighbours),
                (vertical_in, vertical),
                (tracers_in, tracers),
            )
        )
    ]
    for copy in copies:
        copy.start()
    for copy in copies[:2]:
        copy.wait()
    block = jnp.concatenate(
        [
            east[...],
            north[...],
            jnp.broadcast_to(mixing[...].astype(jnp.float32), (16, S)).astype(jnp.bfloat16),
        ],
        0,
    )
    for j in range(LEVELS):
        flow_out[j] = block
    for copy in copies[2:]:
        copy.wait()
    tile = lax.axis_index("tile")
    depth = depths[tile]

    for k in range(LEVELS):
        wet = (k < depth).astype(jnp.float32)
        levels_out[k : k + 1] = jnp.full((1, S), wet, jnp.float32)
        levels_out[LEVELS + k : LEVELS + k + 1] = jnp.full((1, S), wet * vertical[k], jnp.float32)
    for p in range(2 * LEVELS):
        start_out[p] = tracers[p] * (p % LEVELS < depth).astype(jnp.float32)
    rims(lambda p: start_out[p], neighbours[1, tile] >= 0, tile, rims_out)


def ghosts(near, tile, received):
    gx, gs, gn = (jnp.zeros((S // 2, S), jnp.float32) for _ in range(3))
    mate, own, other = received
    toward = jnp.where(tile % 2 == 0, 1, -1)
    for steps, x_block, y_block in (
        (1, mate.at[0], mate.at[2]),
        (2, None, own.at[1]),
        (-1, other.at[0], other.at[1]),
        (-2, None, other.at[2]),
    ):
        slot = tile + steps * toward
        if x_block is not None:
            in_row = (slot == near[0]) | (slot == near[1])
            gx = jnp.where(in_row, x_block[...].astype(jnp.float32), gx)
        block = y_block[...].astype(jnp.float32)
        gs = jnp.where(slot == near[2], block, gs)
        gn = jnp.where(slot == near[3], block, gn)
    return jnp.concatenate([gx, pltpu.roll(gx, S // 2, 1)], 0), gs, gn


def dot(a, b):
    return jnp.dot(a, b, preferred_element_type=jnp.float32)


def inner_sums(values, emit):
    own_right = bands_right(iota((S, S), 0), S)
    right = jnp.concatenate([own_right, own_right], 0)
    own_left = bands_left(iota((S, S), 1), iota((S, S), 0))
    left = jnp.concatenate([own_left, own_left], 1)
    for k in range(LEVELS):
        pair = [values(k), values(k + LEVELS)]
        high = [q.astype(jnp.bfloat16) for q in pair]
        low = [(q - h.astype(jnp.float32)).astype(jnp.bfloat16) for q, h in zip(pair, high)]
        rows = jnp.concatenate([jnp.concatenate([h, l], 1) for h, l in zip(high, low)], 0)
        columns = jnp.concatenate([jnp.concatenate([h, l], 0) for h, l in zip(high, low)], 1)
        along_x = dot(rows, right)
        along_y = dot(left, columns)
        for t in range(2):
            z = -2.0 * pair[t]
            if k > 0:
                z = z + values(k - 1 + t * LEVELS)
            if k < LEVELS - 1:
                z = z + values(k + 1 + t * LEVELS)
            emit(k + t * LEVELS, along_x[t * S : (t + 1) * S], along_y[:, t * S : (t + 1) * S], z)


def rim_sums(near, tile, received):
    gx, gs, gn = ghosts(near, tile, received)
    base = jnp.where(near[1] >= 0, S, -4)
    right = jnp.concatenate([bands_right(iota((8, S), 0) % 4 + base, 8)] * (S // 8), 0)
    row = iota((16, 16), 0)
    row = jnp.where(row < 8, row, row + S - 16)
    column = iota((16, 16), 1)
    source = jnp.where(column < 8, column % 4 - 4, column % 4 + S)
    left = [
        bands_left(jnp.where((column // 4) % 2 == odd, source, -2 * S), row) for odd in range(2)
    ]
    lane_block = iota((S, S), 1) // 4

    def level(k):
        planes = (k, k + LEVELS)
        x_rims = [jnp.where(lane_block == p, gx, 0.0).astype(jnp.bfloat16) for p in planes]
        y_rims = [
            jnp.concatenate([g[8 * (p // 2) : 8 * (p // 2) + 8] for g in (gs, gn)], 0)
            for p in planes
        ]
        along_x = dot(jnp.concatenate(x_rims, 0), right)
        along_y = dot(left[k % 2], jnp.concatenate(y_rims, 1).astype(jnp.bfloat16))
        return [
            (along_x[t * S : (t + 1) * S], along_y[:, t * S : (t + 1) * S]) for t in range(2)
        ]

    return level


def flow_of(flow, k):
    u = flow[k, :S].astype(jnp.float32)
    v = flow[k, S : 2 * S].astype(jnp.float32)
    return u, v, flow[k, 2 * S : 2 * S + 16].astype(jnp.float32)[:1]


def inner_change(u, v, mixing, x_ahead, x_behind, y_ahead, y_behind, curve):
    carry = u * jnp.where(u >= 0, x_ahead, x_behind) + v * jnp.where(v >= 0, y_ahead, y_behind)
    return mixing * curve - carry * (1.0 / 60.0)


def rim_change(u, v, mixing, x, y):
    x_part = mixing * x[:, 2 * S :] - u * jnp.where(u >= 0, x[:, :S], x[:, S : 2 * S]) * (1.0 / 60.0)

    def ends(first, at):
        w = v[at : at + 8]
        slope = jnp.where(w >= 0, y[first : first + 8], y[16 + first : 24 + first])
        return x_part[at : at + 8] + (
            mixing * y[32 + first : 40 + first] - w * slope * (1.0 / 60.0)
        )

    return jnp.concatenate([ends(0, 0), x_part[8 : S - 8], ends(8, S - 8)], 0)


def wet_of(levels, k):
    return levels[k : k + 1]


def lift_of(levels, k):
    return levels[LEVELS + k : LEVELS + k + 1]


def section_kernel(start, flow, levels, neighbours, mate, own, other, section, rims_out):
    tile = lax.axis_index("tile")
    near = beside(neighbours, tile)
    level = rim_sums(near, tile, (mate, own, other))
    rim_parts = {}

    def emit(p, x, y, z):
        k = p % LEVELS
        u, v, mixing = flow_of(flow, k)
        if p < LEVELS:
            rim_parts[p], rim_parts[p + LEVELS] = level(k)
        curve = x[:, 2 * S :] + y[2 * S :]
        change = inner_change(
            u, v, mixing, x[:, :S], x[:, S : 2 * S], y[:S], y[S : 2 * S], curve
        )
        change = change + rim_change(u, v, mixing, *rim_parts[p])
        section[p] = start[p] + (wet_of(levels, k) * change + lift_of(levels, k) * z)

    inner_sums(lambda p: start[p], emit)
    rims(lambda p: section[p], near[1] >= 0, tile, rims_out)


def inner_kernel(start, section, flow, levels, after, out):
    def emit(p, x, y, z):
        k = p % LEVELS
        u, v, mixing = flow_of(flow, k)
        curve = x[:, 2 * S :] + y[2 * S :]
        change = inner_change(
            u, v, mixing, x[:, :S], x[:, S : 2 * S], y[:S], y[S : 2 * S], curve
        )
        change = wet_of(levels, k) * change + lift_of(levels, k) * z
        out[p] = 0.5 * (start[p] + section[p] + change)

    inner_sums(lambda p: section[p], emit)


def last_kernel(inner, flow, levels, neighbours, mate, own, other, out, held, sent):
    tile = lax.axis_index("tile")
    near = beside(neighbours, tile)
    level = rim_sums(near, tile, (mate, own, other))
    copies = []
    for k in range(LEVELS):
        u, v, mixing = flow_of(flow, k)
        for t, (x, y) in enumerate(level(k)):
            p = k + t * LEVELS
            change = rim_change(u, v, mixing, x, y)
            held[p] = inner[p] + (0.5 * wet_of(levels, k)) * change
            copies.append(pltpu.make_async_copy(held.at[p], out.at[p], sent.at[p]))
            copies[-1].start()
    for copy in copies:
        copy.wait()


VMEM = pl.BlockSpec(memory_space=pltpu.VMEM)
SMEM = pl.BlockSpec(memory_space=pltpu.SMEM)
HBM = pl.BlockSpec(memory_space=pltpu.HBM)
ANY = pl.BlockSpec(memory_space=pl.ANY)
PARAMS = pltpu.CompilerParams(vmem_limit_bytes=24 * 1024 * 1024)
COST = pl.CostEstimate(flops=2 * 10**9, bytes_accessed=8 * 10**6, transcendentals=0)
FIELD = pltpu.VMEM((2 * LEVELS, S, S), jnp.float32)
RIMS = pltpu.VMEM((3, S // 2, S), jnp.bfloat16)


def across(mate, blocks):
    return lax.ppermute(jnp.concatenate([mate[:2], blocks[2:]], 0), "tile", ACROSS)


def local(
    tracers, east_velocity, north_velocity, diffusivity, vertical_diffusivity, depths, neighbours
):
    planes = 2 * LEVELS
    neighbours = neighbours.T
    inputs = (
        tracers.reshape(planes, S, S),
        east_velocity.reshape(S, S),
        north_velocity.reshape(S, S),
        diffusivity,
        depths,
        neighbours,
        vertical_diffusivity,
    )
    flow, blocks, start, levels = pl.pallas_call(
        first_kernel,
        out_shape=[
            pltpu.VMEM((LEVELS, 2 * S + 16, S), jnp.bfloat16),
            RIMS,
            FIELD,
            pltpu.VMEM((2 * LEVELS, S), jnp.float32),
        ],
        in_specs=[HBM] * 3 + [VMEM] + [HBM] * 3,
        out_specs=[VMEM] * 4,
        scratch_shapes=[
            pltpu.VMEM((planes, S, S), jnp.float32),
            pltpu.VMEM((S, S), jnp.bfloat16),
            pltpu.VMEM((S, S), jnp.bfloat16),
            pltpu.SMEM((TILES,), jnp.int32),
            pltpu.SMEM((4, TILES), jnp.int32),
            pltpu.SMEM((LEVELS,), jnp.float32),
            pltpu.SemaphoreType.DMA((6,)),
        ],
        compiler_params=PARAMS,
        name="rims",
    )(*(x if x is diffusivity else pltpu.with_memory_space_constraint(x, pltpu.HBM) for x in inputs))
    mate = lax.ppermute(blocks, "tile", MATES)
    flow = lax.all_to_all(flow, "tracer", 0, 0)
    own = across(mate, blocks)
    other = lax.ppermute(own, "tile", MATES)
    section, blocks = pl.pallas_call(
        section_kernel,
        out_shape=[FIELD, RIMS],
        in_specs=[VMEM] * 3 + [SMEM] + [VMEM] * 3,
        out_specs=[VMEM] * 2,
        compiler_params=PARAMS,
        name="section",
    )(start, flow, levels, neighbours, mate, own, other)
    mate = lax.ppermute(blocks, "tile", MATES)
    own = across(mate, blocks)
    inner = pl.pallas_call(
        inner_kernel,
        out_shape=FIELD,
        in_specs=[VMEM] * 4 + [ANY],
        out_specs=VMEM,
        compiler_params=PARAMS,
        cost_estimate=COST,
        name="inner",
    )(start, section, flow, levels, mate)
    own, inner = lax.optimization_barrier((own, inner))
    other = lax.ppermute(own, "tile", MATES)
    out = pl.pallas_call(
        last_kernel,
        out_shape=jax.ShapeDtypeStruct((planes, S, S), jnp.float32),
        in_specs=[VMEM] * 3 + [SMEM] + [VMEM] * 3,
        out_specs=HBM,
        scratch_shapes=[
            pltpu.VMEM((planes, S, S), jnp.float32),
            pltpu.SemaphoreType.DMA((planes,)),
        ],
        compiler_params=PARAMS,
        name="transported",
    )(inner, flow, levels, neighbours, mate, own, other)
    return out.reshape(tracers.shape)


def solution(mesh):
    return jax.shard_map(
        local,
        mesh=mesh,
        in_specs=(
            P("tracer", "tile", None, None, None),
            P("tile", "tracer", None, None),
            P("tile", "tracer", None, None),
            P("tile", "tracer"),
            P(),
            P(),
            P(),
        ),
        out_specs=P("tracer", "tile", None, None, None),
        check_vma=False,
    )
```

```python
import jax
import jax.numpy as jnp
from jax import lax
from jax.experimental import pallas as pl
from jax.experimental.pallas import tpu as pltpu
from jax.sharding import PartitionSpec as P

S = 128
LEVELS = 8
TILES = 32
AHEAD = (-2.0, 15.0, -60.0, 20.0, 30.0, -3.0, 0.0)
BEHIND = (0.0, 3.0, -30.0, -20.0, 60.0, -15.0, 2.0)
CURVE = (0.0, 0.0, 1.0, -2.0, 1.0, 0.0, 0.0)
BANDS = (AHEAD, BEHIND, CURVE)

MATES = [(s, s ^ 1) for s in range(TILES)]
PAIRS = [(s, s + 2) for s in range(TILES - 2) if s % 4 in (0, 3)]
ACROSS = PAIRS + [(t, s) for s, t in PAIRS]


def looks_up(tile):
    return (tile % 4 == 0) | (tile % 4 == 3)


def beside(neighbours, tile):
    row = [neighbours[e, tile] for e in range(4)]
    return [jnp.where(slot < 0, -9, slot) for slot in row]


def band(distance, coefficients):
    total = jnp.zeros(distance.shape, jnp.float32)
    for step, coefficient in zip(range(-3, 4), coefficients):
        if coefficient:
            total = jnp.where(distance == step, coefficient, total)
    return total


def iota(shape, dim):
    return lax.broadcasted_iota(jnp.int32, shape, dim)


def bands_right(source, width):
    out = iota((width, S), 1)
    return jnp.concatenate([band(source - out, c) for c in BANDS], 1).astype(jnp.bfloat16)


def bands_left(source, out):
    return jnp.concatenate([band(source - out, c) for c in BANDS], 0).astype(jnp.bfloat16)


def rims(read, side_east, tile, out):
    planes = 2 * LEVELS
    lane = iota((S, S), 1)
    shift = jnp.where(side_east, 4, 0)
    x_rim = jnp.zeros((S, S), jnp.float32)
    for p in range(planes):
        x_rim = jnp.where(lane // 4 == p, pltpu.roll(read(p), shift + 4 * p, 1), x_rim)
    half = S // 2
    x_rim = jnp.where(lane[:half] < half, x_rim[:half], pltpu.roll(x_rim[half:], half, 1))
    low = iota((8, S), 0) < 4
    south, north = [], []
    for p in range(0, planes, 2):
        first, second = read(p), read(p + 1)
        south.append(jnp.where(low, first[:8], pltpu.roll(second[:8], 4, 0)))
        north.append(jnp.where(low, pltpu.roll(first[S - 8 :], 4, 0), second[S - 8 :]))
    south, north = jnp.concatenate(south, 0), jnp.concatenate(north, 0)
    up = looks_up(tile)
    out[0] = x_rim.astype(jnp.bfloat16)
    out[1] = jnp.where(up, south, north).astype(jnp.bfloat16)
    out[2] = jnp.where(up, north, south).astype(jnp.bfloat16)


def first_kernel(
    tracers_in,
    east_in,
    north_in,
    mixing,
    depths_in,
    neighbours_in,
    vertical_in,
    flow_out,
    rims_out,
    start_out,
    levels_out,
    tracers,
    east,
    north,
    depths,
    neighbours,
    vertical,
    arrived,
):
    copies = [
        pltpu.make_async_copy(source, target, arrived.at[i])
        for i, (source, target) in enumerate(
            (
                (east_in, east),
                (north_in, north),
                (depths_in, depths),
                (neighbours_in, neighbours),
                (vertical_in, vertical),
                (tracers_in, tracers),
            )
        )
    ]
    for copy in copies:
        copy.start()
    for copy in copies[:2]:
        copy.wait()
    block = jnp.concatenate(
        [
            east[...],
            north[...],
            jnp.broadcast_to(mixing[...].astype(jnp.float32), (16, S)).astype(jnp.bfloat16),
        ],
        0,
    )
    for j in range(LEVELS):
        flow_out[j] = block
    for copy in copies[2:]:
        copy.wait()
    tile = lax.axis_index("tile")
    depth = depths[tile]

    for k in range(LEVELS):
        wet = (k < depth).astype(jnp.float32)
        levels_out[k : k + 1] = jnp.full((1, S), wet, jnp.float32)
        levels_out[LEVELS + k : LEVELS + k + 1] = jnp.full((1, S), wet * vertical[k], jnp.float32)
    for p in range(2 * LEVELS):
        start_out[p] = tracers[p] * (p % LEVELS < depth).astype(jnp.float32)
    rims(lambda p: start_out[p], neighbours[1, tile] >= 0, tile, rims_out)


def ghosts(near, tile, received):
    gx, gs, gn = (jnp.zeros((S // 2, S), jnp.float32) for _ in range(3))
    mate, own, other = received
    chip = tile // 2
    for steps in (-2, -1, 1, 2):
        slot = tile + steps
        from_chip = (tile + 2 * TILES + steps) // 2 - TILES
        is_mate = from_chip == chip
        is_own = (from_chip > chip) == looks_up(tile)
        pair = jnp.minimum(from_chip, chip)
        y_at = jnp.where((slot - pair) % 2 == 0, 2, 1)
        if abs(steps) == 1:
            in_row = (slot == near[0]) | (slot == near[1])
            block = jnp.where(is_own, own[0], other[0])
            block = jnp.where(is_mate, mate[0], block)
            gx = jnp.where(in_row, block.astype(jnp.float32), gx)
            mate_y = jnp.where(tile % 4 < 2, mate[2], mate[1])
            block = jnp.where(is_mate, mate_y, jnp.where(is_own, own[y_at], other[y_at]))
        else:
            block = jnp.where(is_own, own[y_at], other[y_at])
        block = block.astype(jnp.float32)
        gs = jnp.where(slot == near[2], block, gs)
        gn = jnp.where(slot == near[3], block, gn)
    return jnp.concatenate([gx, pltpu.roll(gx, S // 2, 1)], 0), gs, gn


def dot(a, b):
    return jnp.dot(a, b, preferred_element_type=jnp.float32)


def inner_sums(values, emit):
    own_right = bands_right(iota((S, S), 0), S)
    right = jnp.concatenate([own_right, own_right], 0)
    own_left = bands_left(iota((S, S), 1), iota((S, S), 0))
    left = jnp.concatenate([own_left, own_left], 1)
    for k in range(LEVELS):
        pair = [values(k), values(k + LEVELS)]
        high = [q.astype(jnp.bfloat16) for q in pair]
        low = [(q - h.astype(jnp.float32)).astype(jnp.bfloat16) for q, h in zip(pair, high)]
        rows = jnp.concatenate([jnp.concatenate([h, l], 1) for h, l in zip(high, low)], 0)
        columns = jnp.concatenate([jnp.concatenate([h, l], 0) for h, l in zip(high, low)], 1)
        along_x = dot(rows, right)
        along_y = dot(left, columns)
        for t in range(2):
            z = -2.0 * pair[t]
            if k > 0:
                z = z + values(k - 1 + t * LEVELS)
            if k < LEVELS - 1:
                z = z + values(k + 1 + t * LEVELS)
            emit(k + t * LEVELS, along_x[t * S : (t + 1) * S], along_y[:, t * S : (t + 1) * S], z)


def rim_sums(near, tile, received):
    gx, gs, gn = ghosts(near, tile, received)
    base = jnp.where(near[1] >= 0, S, -4)
    right = jnp.concatenate([bands_right(iota((8, S), 0) % 4 + base, 8)] * (S // 8), 0)
    row = iota((16, 16), 0)
    row = jnp.where(row < 8, row, row + S - 16)
    column = iota((16, 16), 1)
    source = jnp.where(column < 8, column % 4 - 4, column % 4 + S)
    left = [
        bands_left(jnp.where((column // 4) % 2 == odd, source, -2 * S), row) for odd in range(2)
    ]
    lane_block = iota((S, S), 1) // 4

    def level(k):
        planes = (k, k + LEVELS)
        x_rims = [jnp.where(lane_block == p, gx, 0.0).astype(jnp.bfloat16) for p in planes]
        y_rims = [
            jnp.concatenate([g[8 * (p // 2) : 8 * (p // 2) + 8] for g in (gs, gn)], 0)
            for p in planes
        ]
        along_x = dot(jnp.concatenate(x_rims, 0), right)
        along_y = dot(left[k % 2], jnp.concatenate(y_rims, 1).astype(jnp.bfloat16))
        return [
            (along_x[t * S : (t + 1) * S], along_y[:, t * S : (t + 1) * S]) for t in range(2)
        ]

    return level


def flow_of(flow, k):
    u = flow[k, :S].astype(jnp.float32)
    v = flow[k, S : 2 * S].astype(jnp.float32)
    return u, v, flow[k, 2 * S : 2 * S + 16].astype(jnp.float32)[:1]


def inner_change(u, v, mixing, x_ahead, x_behind, y_ahead, y_behind, curve):
    carry = u * jnp.where(u >= 0, x_ahead, x_behind) + v * jnp.where(v >= 0, y_ahead, y_behind)
    return mixing * curve - carry * (1.0 / 60.0)


def rim_change(u, v, mixing, x, y):
    x_part = mixing * x[:, 2 * S :] - u * jnp.where(u >= 0, x[:, :S], x[:, S : 2 * S]) * (1.0 / 60.0)

    def ends(first, at):
        w = v[at : at + 8]
        slope = jnp.where(w >= 0, y[first : first + 8], y[16 + first : 24 + first])
        return x_part[at : at + 8] + (
            mixing * y[32 + first : 40 + first] - w * slope * (1.0 / 60.0)
        )

    return jnp.concatenate([ends(0, 0), x_part[8 : S - 8], ends(8, S - 8)], 0)


def wet_of(levels, k):
    return levels[k : k + 1]


def lift_of(levels, k):
    return levels[LEVELS + k : LEVELS + k + 1]


def section_kernel(start, flow, levels, neighbours, mate, own, other, section, rims_out):
    tile = lax.axis_index("tile")
    near = beside(neighbours, tile)
    level = rim_sums(near, tile, (mate, own, other))
    rim_parts = {}

    def emit(p, x, y, z):
        k = p % LEVELS
        u, v, mixing = flow_of(flow, k)
        if p < LEVELS:
            rim_parts[p], rim_parts[p + LEVELS] = level(k)
        curve = x[:, 2 * S :] + y[2 * S :]
        change = inner_change(
            u, v, mixing, x[:, :S], x[:, S : 2 * S], y[:S], y[S : 2 * S], curve
        )
        change = change + rim_change(u, v, mixing, *rim_parts[p])
        section[p] = start[p] + (wet_of(levels, k) * change + lift_of(levels, k) * z)

    inner_sums(lambda p: start[p], emit)
    rims(lambda p: section[p], near[1] >= 0, tile, rims_out)


def inner_kernel(start, section, flow, levels, after, out):
    def emit(p, x, y, z):
        k = p % LEVELS
        u, v, mixing = flow_of(flow, k)
        curve = x[:, 2 * S :] + y[2 * S :]
        change = inner_change(
            u, v, mixing, x[:, :S], x[:, S : 2 * S], y[:S], y[S : 2 * S], curve
        )
        change = wet_of(levels, k) * change + lift_of(levels, k) * z
        out[p] = 0.5 * (start[p] + section[p] + change)

    inner_sums(lambda p: section[p], emit)


def last_kernel(inner, flow, levels, neighbours, mate, own, other, out, held, sent):
    tile = lax.axis_index("tile")
    near = beside(neighbours, tile)
    level = rim_sums(near, tile, (mate, own, other))
    copies = []
    for k in range(LEVELS):
        u, v, mixing = flow_of(flow, k)
        for t, (x, y) in enumerate(level(k)):
            p = k + t * LEVELS
            change = rim_change(u, v, mixing, x, y)
            held[p] = inner[p] + (0.5 * wet_of(levels, k)) * change
            copies.append(pltpu.make_async_copy(held.at[p], out.at[p], sent.at[p]))
            copies[-1].start()
    for copy in copies:
        copy.wait()


VMEM = pl.BlockSpec(memory_space=pltpu.VMEM)
SMEM = pl.BlockSpec(memory_space=pltpu.SMEM)
HBM = pl.BlockSpec(memory_space=pltpu.HBM)
ANY = pl.BlockSpec(memory_space=pl.ANY)
PARAMS = pltpu.CompilerParams(vmem_limit_bytes=24 * 1024 * 1024)
COST = pl.CostEstimate(flops=2 * 10**9, bytes_accessed=8 * 10**6, transcendentals=0)
FIELD = pltpu.VMEM((2 * LEVELS, S, S), jnp.float32)
RIMS = pltpu.VMEM((3, S // 2, S), jnp.bfloat16)


def across(mate, blocks):
    tile = lax.axis_index("tile")
    x_rim = jnp.where(tile % 4 < 2, mate[:1], blocks[:1])
    return lax.ppermute(jnp.concatenate([x_rim, mate[1:2], blocks[2:]], 0), "tile", ACROSS)


def local(
    tracers, east_velocity, north_velocity, diffusivity, vertical_diffusivity, depths, neighbours
):
    planes = 2 * LEVELS
    neighbours = neighbours.T
    inputs = (
        tracers.reshape(planes, S, S),
        east_velocity.reshape(S, S),
        north_velocity.reshape(S, S),
        diffusivity,
        depths,
        neighbours,
        vertical_diffusivity,
    )
    flow, blocks, start, levels = pl.pallas_call(
        first_kernel,
        out_shape=[
            pltpu.VMEM((LEVELS, 2 * S + 16, S), jnp.bfloat16),
            RIMS,
            FIELD,
            pltpu.VMEM((2 * LEVELS, S), jnp.float32),
        ],
        in_specs=[HBM] * 3 + [VMEM] + [HBM] * 3,
        out_specs=[VMEM] * 4,
        scratch_shapes=[
            pltpu.VMEM((planes, S, S), jnp.float32),
            pltpu.VMEM((S, S), jnp.bfloat16),
            pltpu.VMEM((S, S), jnp.bfloat16),
            pltpu.SMEM((TILES,), jnp.int32),
            pltpu.SMEM((4, TILES), jnp.int32),
            pltpu.SMEM((LEVELS,), jnp.float32),
            pltpu.SemaphoreType.DMA((6,)),
        ],
        compiler_params=PARAMS,
        name="rims",
    )(*(x if x is diffusivity else pltpu.with_memory_space_constraint(x, pltpu.HBM) for x in inputs))
    mate = lax.ppermute(blocks, "tile", MATES)
    flow = lax.all_to_all(flow, "tracer", 0, 0)
    own = across(mate, blocks)
    other = lax.ppermute(own, "tile", MATES)
    section, blocks = pl.pallas_call(
        section_kernel,
        out_shape=[FIELD, RIMS],
        in_specs=[VMEM] * 3 + [SMEM] + [VMEM] * 3,
        out_specs=[VMEM] * 2,
        compiler_params=PARAMS,
        name="section",
    )(start, flow, levels, neighbours, mate, own, other)
    mate = lax.ppermute(blocks, "tile", MATES)
    own = across(mate, blocks)
    inner = pl.pallas_call(
        inner_kernel,
        out_shape=FIELD,
        in_specs=[VMEM] * 4 + [ANY],
        out_specs=VMEM,
        compiler_params=PARAMS,
        cost_estimate=COST,
        name="inner",
    )(start, section, flow, levels, mate)
    own, inner = lax.optimization_barrier((own, inner))
    other = lax.ppermute(own, "tile", MATES)
    out = pl.pallas_call(
        last_kernel,
        out_shape=jax.ShapeDtypeStruct((planes, S, S), jnp.float32),
        in_specs=[VMEM] * 3 + [SMEM] + [VMEM] * 3,
        out_specs=HBM,
        scratch_shapes=[
            pltpu.VMEM((planes, S, S), jnp.float32),
            pltpu.SemaphoreType.DMA((planes,)),
        ],
        compiler_params=PARAMS,
        name="transported",
    )(inner, flow, levels, neighbours, mate, own, other)
    return out.reshape(tracers.shape)


def solution(mesh):
    return jax.shard_map(
        local,
        mesh=mesh,
        in_specs=(
            P("tracer", "tile", None, None, None),
            P("tile", "tracer", None, None),
            P("tile", "tracer", None, None),
            P("tile", "tracer"),
            P(),
            P(),
            P(),
        ),
        out_specs=P("tracer", "tile", None, None, None),
        check_vma=False,
    )
```

```python
import jax
import jax.numpy as jnp
from jax import lax
from jax.experimental import pallas as pl
from jax.experimental.pallas import tpu as pltpu
from jax.sharding import PartitionSpec as P

S = 128
LEVELS = 8
TILES = 32
AHEAD = (-2.0, 15.0, -60.0, 20.0, 30.0, -3.0, 0.0)
BEHIND = (0.0, 3.0, -30.0, -20.0, 60.0, -15.0, 2.0)
CURVE = (0.0, 0.0, 1.0, -2.0, 1.0, 0.0, 0.0)
BANDS = (AHEAD, BEHIND, CURVE)

MATES = [(s, s ^ 1) for s in range(TILES)]
PAIRS = [(s, s + 2) for s in range(TILES - 2) if s % 4 in (0, 3)]
ACROSS = PAIRS + [(t, s) for s, t in PAIRS]


def looks_up(tile):
    return (tile % 4 == 0) | (tile % 4 == 3)


def beside(neighbours, tile):
    row = [neighbours[e, tile] for e in range(4)]
    return [jnp.where(slot < 0, -9, slot) for slot in row]


def band(distance, coefficients):
    total = jnp.zeros(distance.shape, jnp.float32)
    for step, coefficient in zip(range(-3, 4), coefficients):
        if coefficient:
            total = jnp.where(distance == step, coefficient, total)
    return total


def iota(shape, dim):
    return lax.broadcasted_iota(jnp.int32, shape, dim)


def bands(distance, axis):
    return jnp.concatenate([band(distance, c) for c in BANDS], axis).astype(jnp.bfloat16)


def pack_rims(tile, x_rim, top, bottom, out):
    half = S // 2
    lane = iota((half, S), 1)
    x_rim = jnp.where(lane < half, x_rim[:half], pltpu.roll(x_rim[half:], half, 1))
    low = iota((8, S), 0) < 4
    south, north = [], []
    for p in range(0, 2 * LEVELS, 2):
        south.append(jnp.where(low, top(p), pltpu.roll(top(p + 1), 4, 0)))
        north.append(jnp.where(low, pltpu.roll(bottom(p), 4, 0), bottom(p + 1)))
    south, north = jnp.concatenate(south, 0), jnp.concatenate(north, 0)
    up = looks_up(tile)
    out[0] = x_rim.astype(jnp.bfloat16)
    out[1] = jnp.where(up, south, north).astype(jnp.bfloat16)
    out[2] = jnp.where(up, north, south).astype(jnp.bfloat16)


def rims(field, side_east, tile, out):
    lane = iota((S, S), 1)
    shift = jnp.where(side_east, 4, 0)
    x_rim = jnp.zeros((S, S), jnp.float32)
    for p in range(2 * LEVELS):
        x_rim = jnp.where(lane // 4 == p, pltpu.roll(field[p], shift + 4 * p, 1), x_rim)
    pack_rims(tile, x_rim, lambda p: field[p, :8], lambda p: field[p, S - 8 :], out)


def first_kernel(
    tracers_in,
    east_in,
    north_in,
    mixing,
    depths_in,
    neighbours_in,
    vertical_in,
    flow_out,
    rims_out,
    start_out,
    levels_out,
    tracers,
    east,
    north,
    depths,
    neighbours,
    vertical,
    block,
    arrived,
    sent,
):
    copies = [
        pltpu.make_async_copy(source, target, arrived.at[i])
        for i, (source, target) in enumerate(
            (
                (east_in, east),
                (north_in, north),
                (depths_in, depths),
                (neighbours_in, neighbours),
                (vertical_in, vertical),
                (tracers_in, tracers),
            )
        )
    ]
    for copy in copies:
        copy.start()
    for copy in copies[:2]:
        copy.wait()
    block[:S] = east[...]
    block[S : 2 * S] = north[...]
    last = jnp.broadcast_to(mixing[...].astype(jnp.float32), (16, S))
    block[2 * S :] = last.astype(jnp.bfloat16)
    leaving = [pltpu.make_async_copy(block, flow_out.at[j], sent.at[j]) for j in range(LEVELS)]
    for copy in leaving:
        copy.start()
    for copy in copies[2:]:
        copy.wait()
    tile = lax.axis_index("tile")
    depth = depths[tile]

    for k in range(LEVELS):
        wet = (k < depth).astype(jnp.float32)
        levels_out[k : k + 1] = jnp.full((1, S), wet, jnp.float32)
        levels_out[LEVELS + k : LEVELS + k + 1] = jnp.full((1, S), wet * vertical[k], jnp.float32)
    for p in range(2 * LEVELS):
        start_out[p] = tracers[p] * (p % LEVELS < depth).astype(jnp.float32)
    rims(start_out, neighbours[1, tile] >= 0, tile, rims_out)
    for copy in leaving:
        copy.wait()


def ghosts(near, tile, received):
    gx, gs, gn = (jnp.zeros((S // 2, S), jnp.float32) for _ in range(3))
    mate, own, other = received
    chip = tile // 2
    for steps in (-2, -1, 1, 2):
        slot = tile + steps
        from_chip = (tile + 2 * TILES + steps) // 2 - TILES
        is_mate = from_chip == chip
        is_own = (from_chip > chip) == looks_up(tile)
        pair = jnp.minimum(from_chip, chip)
        y_at = jnp.where((slot - pair) % 2 == 0, 2, 1)
        if abs(steps) == 1:
            in_row = (slot == near[0]) | (slot == near[1])
            block = jnp.where(is_own, own[0], other[0])
            block = jnp.where(is_mate, mate[0], block)
            gx = jnp.where(in_row, block.astype(jnp.float32), gx)
            mate_y = jnp.where(tile % 4 < 2, mate[2], mate[1])
            block = jnp.where(is_mate, mate_y, jnp.where(is_own, own[y_at], other[y_at]))
        else:
            block = jnp.where(is_own, own[y_at], other[y_at])
        block = block.astype(jnp.float32)
        gs = jnp.where(slot == near[2], block, gs)
        gn = jnp.where(slot == near[3], block, gn)
    return jnp.concatenate([gx, pltpu.roll(gx, S // 2, 1)], 0), gs, gn


def dot(a, b):
    return jnp.dot(a, b, preferred_element_type=jnp.float32)


def split(q):
    high = q.astype(jnp.bfloat16)
    return high, (q - high.astype(jnp.float32)).astype(jnp.bfloat16)


def inner_sums(values, right, left, emit):
    for k in range(LEVELS):
        pair = [values(k), values(k + LEVELS)]
        parts = [split(q) for q in pair]
        along_x = dot(jnp.concatenate([jnp.concatenate(q, 1) for q in parts], 0), right[...])
        along_y = dot(left[...], jnp.concatenate([jnp.concatenate(q, 0) for q in parts], 1))
        for t in range(2):
            z = second_difference(values, k + t * LEVELS)
            emit(k + t * LEVELS, along_x[t * S : (t + 1) * S], along_y[:, t * S : (t + 1) * S], z)


def second_difference(values, p):
    z = -2.0 * values(p)
    if p % LEVELS > 0:
        z = z + values(p - 1)
    if p % LEVELS < LEVELS - 1:
        z = z + values(p + 1)
    return z


def rim_changes(near, tile, received, flow, along, right_rim_packed, left_rim):
    gx, gs, gn = ghosts(near, tile, received)
    sums = dot(gx.astype(jnp.bfloat16), right_rim_packed[...])
    u = along[:S]
    change = carried(u, along[S : S + 1], sums[:, :S], sums[:, S : 2 * S], sums[:, 2 * S :])
    packed = along[S + 8 : S + 9] * change
    side_east = near[1] >= 0
    lane = iota((S, S), 1)
    window = lane - jnp.where(side_east, S - 8, 0)
    in_window = (window >= 0) & (window < 8)
    back = jnp.where(side_east, S - 8, S)

    def rows(p):
        return jnp.where(in_window, pltpu.roll(packed, back - 8 * p, 1), 0.0)

    sums_y = []
    for odd in range(2):
        y_rims = [
            jnp.concatenate([gs[8 * t : 8 * t + 8], gn[8 * t : 8 * t + 8]], 0)
            for t in range(LEVELS)
        ]
        sums_y.append(dot(left_rim[odd], jnp.concatenate(y_rims, 1).astype(jnp.bfloat16)))

    def ends(p):
        _, v, mixing = flow_of(flow, p % LEVELS)
        v = jnp.concatenate([v[:8], v[S - 8 :]], 0)
        y = sums_y[p % 2][:, S * (p // 2) : S * (p // 2 + 1)]
        return carried(v, mixing, y[:16], y[16:32], y[32:])

    return rows, ends


def add_ends(plane, ends):
    return jnp.concatenate(
        [plane[:8] + ends[:8], plane[8 : S - 8], plane[S - 8 :] + ends[8:]], 0
    )


def bands_kernel(
    start,
    neighbours,
    after,
    columns,
    right,
    left,
    right_rim,
    left_rim,
    right_packed,
    right_rim_packed,
    left_edge,
    left_rim_packed,
    repack,
):
    tile = lax.axis_index("tile")
    side_east = neighbours[1, tile] >= 0
    row, lane = iota((S, S), 0), iota((S, S), 1)
    own = bands(row - lane, 1)
    right[...] = jnp.concatenate([own, own], 0)
    own = bands(lane - row, 0)
    left[...] = jnp.concatenate([own, own], 1)
    base = jnp.where(side_east, S, -4)
    right_rim[...] = bands(row % 4 + base - lane, 1)
    own = bands(jnp.where(row // 8 == lane // 8, row % 8 - lane % 8, S), 1)
    right_packed[...] = jnp.concatenate([own, own], 0)
    base = jnp.where(side_east, 8, -4)
    right_rim_packed[...] = bands(
        jnp.where(row // 4 == lane // 8, row % 4 + base - lane % 8, S), 1
    )
    at = row % 8 - jnp.where(side_east, 4, 0)
    moves = (row // 8 == lane // 4) & (at == lane % 4)
    repack[...] = jnp.where(moves, 1.0, 0.0).astype(jnp.bfloat16)
    out = iota((16, 48), 0)
    out = jnp.where(out < 8, out, out + S - 16)
    column = iota((16, 48), 1)
    cell = column % 16
    same = jnp.where(cell < 8, cell, cell + S - 16)
    rim = jnp.where(cell < 8, cell % 4 - 4, cell % 4 + S)
    for odd in range(2):
        mine = jnp.where((cell // 4) % 2 == odd, rim, -2 * S)
        left_edge[odd] = bands(jnp.where(column < 32, same, mine) - out, 0)
        left_rim[odd] = bands(mine[:, :16] - out[:, :16], 0)
    cell = column[:, :16]
    both = jnp.where(cell < 4, cell - 4, jnp.where(cell < 8, cell + S - 4, -2 * S))
    left_rim_packed[...] = bands(both - out[:, :16], 0)
    packed = jnp.zeros((S, S), jnp.float32)
    shift = jnp.where(side_east, 8, 0)
    for p in range(2 * LEVELS):
        packed = jnp.where(lane // 8 == p, pltpu.roll(start[p], shift + 8 * p, 1), packed)
    columns[...] = packed


def flow_of(flow, k):
    u = flow[k, :S].astype(jnp.float32)
    v = flow[k, S : 2 * S].astype(jnp.float32)
    return u, v, flow[k, 2 * S : 2 * S + 16].astype(jnp.float32)[:1]


def inner_change(u, v, mixing, x_ahead, x_behind, y_ahead, y_behind, curve):
    carry = u * jnp.where(u >= 0, x_ahead, x_behind) + v * jnp.where(v >= 0, y_ahead, y_behind)
    return mixing * curve - carry * (1.0 / 60.0)


def carried(flow, mixing, ahead, behind, curve):
    return mixing * curve - flow * jnp.where(flow >= 0, ahead, behind) * (1.0 / 60.0)


def wet_of(levels, k):
    return levels[k : k + 1]


def lift_of(levels, k):
    return levels[LEVELS + k : LEVELS + k + 1]


def edge_kernel(
    start,
    columns,
    flow,
    levels,
    neighbours,
    mate,
    own,
    other,
    right,
    right_rim,
    left,
    right_packed,
    right_rim_packed,
    left_edge,
    left_rim_packed,
    repack,
    rims_out,
    along_out,
):
    tile = lax.axis_index("tile")
    near = beside(neighbours, tile)
    gx, gs, gn = ghosts(near, tile, (mate, own, other))
    planes = 2 * LEVELS

    shift = jnp.where(near[1] >= 0, 8, 0)
    block = iota((S, S), 1) // 8
    u_packed = jnp.zeros((S, S), jnp.float32)
    v_packed = jnp.zeros((S, S), jnp.float32)
    row_block = block[:1] % LEVELS
    mixing, wet, lift = (jnp.zeros((1, S), jnp.float32) for _ in range(3))
    for k in range(LEVELS):
        u, v, m = flow_of(flow, k)
        u_packed = jnp.where(block == k, pltpu.roll(u, shift + 8 * k, 1), u_packed)
        v_packed = jnp.where(block == k, pltpu.roll(v, shift + 8 * k, 1), v_packed)
        mixing = jnp.where(row_block == k, m, mixing)
        wet = jnp.where(row_block == k, wet_of(levels, k), wet)
        lift = jnp.where(row_block == k, lift_of(levels, k), lift)
    u_packed = jnp.where(block < LEVELS, u_packed, pltpu.roll(u_packed, S // 2, 1))
    v_packed = jnp.where(block < LEVELS, v_packed, pltpu.roll(v_packed, S // 2, 1))
    along_out[:S] = u_packed
    along_out[S : S + 8] = jnp.broadcast_to(mixing, (8, S))
    along_out[S + 8 :] = jnp.broadcast_to(wet, (8, S))
    low = iota((8, S), 0) < 4
    rim = jnp.zeros((8, S), jnp.float32)
    for p in range(planes):
        at = 8 * (p // 2)
        pair = (gs[at : at + 8], gn[at : at + 8])
        if p % 2:
            both = jnp.where(low, pltpu.roll(pair[0], 4, 0), pair[1])
        else:
            both = jnp.where(low, pair[0], pltpu.roll(pair[1], 4, 0))
        rim = jnp.where(block[:8] == p, pltpu.roll(both, shift + 8 * p, 1), rim)
    rim = jnp.concatenate([rim, jnp.zeros_like(rim)], 0).astype(jnp.bfloat16)
    q = columns[...]
    parts = split(q)
    x = dot(jnp.concatenate(parts, 1), right_packed[...])
    x = x + dot(gx.astype(jnp.bfloat16), right_rim_packed[...])
    y = dot(left[...], jnp.concatenate(parts, 0))
    y_rim = dot(left_rim_packed[...], rim)
    y = [
        jnp.concatenate(
            [
                y[i * S : i * S + 8] + y_rim[16 * i : 16 * i + 8],
                y[i * S + 8 : (i + 1) * S - 8],
                y[(i + 1) * S - 8 : (i + 1) * S] + y_rim[16 * i + 8 : 16 * i + 16],
            ],
            0,
        )
        for i in range(3)
    ]
    z = -2.0 * q
    z = z + jnp.where(block % LEVELS > 0, pltpu.roll(q, 8, 1), 0.0)
    z = z + jnp.where(block % LEVELS < LEVELS - 1, pltpu.roll(q, S - 8, 1), 0.0)
    change = inner_change(
        u_packed, v_packed, mixing, x[:, :S], x[:, S : 2 * S], y[0], y[1], x[:, 2 * S :] + y[2]
    )
    section = q + (wet * change + lift * z)
    x_rim = dot(section.astype(jnp.bfloat16), repack[...])

    def ends(a):
        return jnp.concatenate([a[:8], a[S - 8 :]], 0)

    values = [jnp.concatenate([start[p, :8], start[p, S - 8 :]], 0) for p in range(planes)]
    parts = [split(q) for q in values]
    gx_ends = ends(gx)
    lane_block = iota((16, S), 1) // 4
    x_rims = [jnp.where(lane_block == p, gx_ends, 0.0) for p in range(planes)]
    x = dot(jnp.concatenate([jnp.concatenate(q, 1) for q in parts], 0), right[...])
    x = x + dot(jnp.concatenate(x_rims, 0).astype(jnp.bfloat16), right_rim[...])
    ys = []
    for odd in range(2):
        sources = []
        for p in range(odd, planes, 2):
            at = 8 * (p // 2)
            y_rims = jnp.concatenate([gs[at : at + 8], gn[at : at + 8]], 0).astype(jnp.bfloat16)
            sources.append(jnp.concatenate([*parts[p], y_rims], 0))
        ys.append(dot(left_edge[odd], jnp.concatenate(sources, 1)))
    sections = []
    for p in range(planes):
        k = p % LEVELS
        u = ends(flow[k, :S].astype(jnp.float32))
        v = ends(flow[k, S : 2 * S].astype(jnp.float32))
        m = flow[k, 2 * S : 2 * S + 16].astype(jnp.float32)
        xp = x[16 * p : 16 * p + 16]
        yp = ys[p % 2][:, S * (p // 2) : S * (p // 2 + 1)]
        change = inner_change(
            u, v, m, xp[:, :S], xp[:, S : 2 * S], yp[:16], yp[16:32], xp[:, 2 * S :] + yp[32:]
        )
        z = second_difference(lambda i: values[i], p)
        sections.append(values[p] + (wet_of(levels, k) * change + lift_of(levels, k) * z))
    pack_rims(tile, x_rim, lambda p: sections[p][:8], lambda p: sections[p][8:], rims_out)


def middle_kernel(
    start,
    flow,
    levels,
    neighbours,
    mate,
    own,
    other,
    right,
    left,
    along,
    right_rim_packed,
    left_rim,
    after,
    out,
    section,
):
    tile = lax.axis_index("tile")
    near = beside(neighbours, tile)
    received = (mate, own, other)
    rows, ends = rim_changes(near, tile, received, flow, along, right_rim_packed, left_rim)

    def inner(p, x, y, z):
        k = p % LEVELS
        u, v, mixing = flow_of(flow, k)
        curve = x[:, 2 * S :] + y[2 * S :]
        change = inner_change(
            u, v, mixing, x[:, :S], x[:, S : 2 * S], y[:S], y[S : 2 * S], curve
        )
        return wet_of(levels, k) * change + lift_of(levels, k) * z

    def first(p, x, y, z):
        plane = start[p] + (inner(p, x, y, z) + rows(p))
        section[p] = add_ends(plane, wet_of(levels, p % LEVELS) * ends(p))

    def second(p, x, y, z):
        out[p] = 0.5 * (start[p] + section[p] + inner(p, x, y, z))

    inner_sums(lambda p: start[p], right, left, first)
    inner_sums(lambda p: section[p], right, left, second)


def last_kernel(
    inner,
    flow,
    levels,
    neighbours,
    mate,
    own,
    other,
    along,
    right_rim_packed,
    left_rim,
    out,
    held,
    sent,
):
    tile = lax.axis_index("tile")
    near = beside(neighbours, tile)
    received = (mate, own, other)
    rows, ends = rim_changes(near, tile, received, flow, along, right_rim_packed, left_rim)
    copies = []
    for p in range(2 * LEVELS):
        plane = inner[p] + 0.5 * rows(p)
        held[p] = add_ends(plane, (0.5 * wet_of(levels, p % LEVELS)) * ends(p))
        copies.append(pltpu.make_async_copy(held.at[p], out.at[p], sent.at[p]))
        copies[-1].start()
    for copy in copies:
        copy.wait()


VMEM = pl.BlockSpec(memory_space=pltpu.VMEM)
SMEM = pl.BlockSpec(memory_space=pltpu.SMEM)
HBM = pl.BlockSpec(memory_space=pltpu.HBM)
ANY = pl.BlockSpec(memory_space=pl.ANY)
PARAMS = pltpu.CompilerParams(vmem_limit_bytes=24 * 1024 * 1024)
COST = pl.CostEstimate(flops=2 * 10**9, bytes_accessed=8 * 10**6, transcendentals=0)
FIELD = pltpu.VMEM((2 * LEVELS, S, S), jnp.float32)
RIMS = pltpu.VMEM((3, S // 2, S), jnp.bfloat16)


def across(mate, blocks):
    tile = lax.axis_index("tile")
    x_rim = jnp.where(tile % 4 < 2, mate[:1], blocks[:1])
    return lax.ppermute(jnp.concatenate([x_rim, mate[1:2], blocks[2:]], 0), "tile", ACROSS)


def local(
    tracers, east_velocity, north_velocity, diffusivity, vertical_diffusivity, depths, neighbours
):
    planes = 2 * LEVELS
    neighbours = neighbours.T
    inputs = (
        tracers.reshape(planes, S, S),
        east_velocity.reshape(S, S),
        north_velocity.reshape(S, S),
        diffusivity,
        depths,
        neighbours,
        vertical_diffusivity,
    )
    flow, blocks, start, levels = pl.pallas_call(
        first_kernel,
        out_shape=[
            pltpu.HBM((LEVELS, 2 * S + 16, S), jnp.bfloat16),
            RIMS,
            FIELD,
            pltpu.VMEM((2 * LEVELS, S), jnp.float32),
        ],
        in_specs=[HBM] * 3 + [VMEM] + [HBM] * 3,
        out_specs=[HBM] + [VMEM] * 3,
        scratch_shapes=[
            pltpu.VMEM((planes, S, S), jnp.float32),
            pltpu.VMEM((S, S), jnp.bfloat16),
            pltpu.VMEM((S, S), jnp.bfloat16),
            pltpu.SMEM((TILES,), jnp.int32),
            pltpu.SMEM((4, TILES), jnp.int32),
            pltpu.SMEM((LEVELS,), jnp.float32),
            pltpu.VMEM((2 * S + 16, S), jnp.bfloat16),
            pltpu.SemaphoreType.DMA((6,)),
            pltpu.SemaphoreType.DMA((LEVELS,)),
        ],
        compiler_params=PARAMS,
        name="rims",
    )(*(x if x is diffusivity else pltpu.with_memory_space_constraint(x, pltpu.HBM) for x in inputs))
    mate = lax.ppermute(blocks, "tile", MATES)
    flow = lax.all_to_all(flow, "tracer", 0, 0)
    own = across(mate, blocks)
    columns, right, left, right_rim, left_rim, *packed = pl.pallas_call(
        bands_kernel,
        out_shape=[pltpu.VMEM((S, S), jnp.float32)]
        + [
            pltpu.VMEM(shape, jnp.bfloat16)
            for shape in (
                (2 * S, 3 * S),
                (3 * S, 2 * S),
                (S, 3 * S),
                (2, 48, 16),
                (2 * S, 3 * S),
                (S, 3 * S),
                (2, 48, 48),
                (48, 16),
                (S, S),
            )
        ],
        in_specs=[VMEM, SMEM, ANY],
        out_specs=[VMEM] * 10,
        compiler_params=PARAMS,
        cost_estimate=COST,
        name="bands",
    )(start, neighbours, mate)
    own, columns = lax.optimization_barrier((own, columns))
    received = mate, own, lax.ppermute(own, "tile", MATES)
    blocks, along = pl.pallas_call(
        edge_kernel,
        out_shape=[RIMS, pltpu.VMEM((S + 16, S), jnp.float32)],
        in_specs=[VMEM] * 4 + [SMEM] + [VMEM] * 11,
        out_specs=[VMEM] * 2,
        compiler_params=PARAMS,
        name="edges",
    )(start, columns, flow, levels, neighbours, *received, right, right_rim, left, *packed)
    mate = lax.ppermute(blocks, "tile", MATES)
    own = across(mate, blocks)
    inner = pl.pallas_call(
        middle_kernel,
        out_shape=FIELD,
        in_specs=[VMEM] * 3 + [SMEM] + [VMEM] * 8 + [ANY],
        out_specs=VMEM,
        scratch_shapes=[pltpu.VMEM((planes, S, S), jnp.float32)],
        compiler_params=PARAMS,
        cost_estimate=COST,
        name="middle",
    )(start, flow, levels, neighbours, *received, right, left, along, packed[1], left_rim, mate)
    own, inner = lax.optimization_barrier((own, inner))
    received = mate, own, lax.ppermute(own, "tile", MATES)
    out = pl.pallas_call(
        last_kernel,
        out_shape=jax.ShapeDtypeStruct((planes, S, S), jnp.float32),
        in_specs=[VMEM] * 3 + [SMEM] + [VMEM] * 6,
        out_specs=HBM,
        scratch_shapes=[
            pltpu.VMEM((planes, S, S), jnp.float32),
            pltpu.SemaphoreType.DMA((planes,)),
        ],
        compiler_params=PARAMS,
        name="transported",
    )(inner, flow, levels, neighbours, *received, along, packed[1], left_rim)
    return out.reshape(tracers.shape)


def solution(mesh):
    return jax.shard_map(
        local,
        mesh=mesh,
        in_specs=(
            P("tracer", "tile", None, None, None),
            P("tile", "tracer", None, None),
            P("tile", "tracer", None, None),
            P("tile", "tracer"),
            P(),
            P(),
            P(),
        ),
        out_specs=P("tracer", "tile", None, None, None),
        check_vma=False,
    )
```

```python
import jax
import jax.numpy as jnp
from jax import lax
from jax.experimental import pallas as pl
from jax.experimental.pallas import tpu as pltpu
from jax.sharding import PartitionSpec as P

S = 128
LEVELS = 8
TILES = 32
AHEAD = (-2.0, 15.0, -60.0, 20.0, 30.0, -3.0, 0.0)
BEHIND = (0.0, 3.0, -30.0, -20.0, 60.0, -15.0, 2.0)
CURVE = (0.0, 0.0, 1.0, -2.0, 1.0, 0.0, 0.0)
BANDS = (AHEAD, BEHIND, CURVE)

MATES = [(s, s ^ 1) for s in range(TILES)]
PAIRS = [(s, s + 2) for s in range(TILES - 2) if s % 4 in (0, 3)]
ACROSS = PAIRS + [(t, s) for s, t in PAIRS]


def looks_up(tile):
    return (tile % 4 == 0) | (tile % 4 == 3)


def beside(levels):
    return [levels[2 * LEVELS + e : 2 * LEVELS + e + 1] for e in range(4)]


def band(distance, coefficients):
    total = jnp.zeros(distance.shape, jnp.float32)
    for step, coefficient in zip(range(-3, 4), coefficients):
        if coefficient:
            total = jnp.where(distance == step, coefficient, total)
    return total


def iota(shape, dim):
    return lax.broadcasted_iota(jnp.int32, shape, dim)


def bands(distance, axis):
    return jnp.concatenate([band(distance, c) for c in BANDS], axis).astype(jnp.bfloat16)


def pack_rims(tile, x_rim, top, bottom, out):
    half = S // 2
    lane = iota((half, S), 1)
    x_rim = jnp.where(lane < half, x_rim[:half], pltpu.roll(x_rim[half:], half, 1))
    low = iota((8, S), 0) < 4
    south, north = [], []
    for p in range(0, 2 * LEVELS, 2):
        south.append(jnp.where(low, top(p), pltpu.roll(top(p + 1), 4, 0)))
        north.append(jnp.where(low, pltpu.roll(bottom(p), 4, 0), bottom(p + 1)))
    south, north = jnp.concatenate(south, 0), jnp.concatenate(north, 0)
    up = looks_up(tile)
    out[0] = x_rim.astype(jnp.bfloat16)
    out[1] = jnp.where(up, south, north).astype(jnp.bfloat16)
    out[2] = jnp.where(up, north, south).astype(jnp.bfloat16)


def rims(field, side_east, tile, out):
    lane = iota((S, S), 1)
    shift = jnp.where(side_east, 4, 0)
    x_rim = jnp.zeros((S, S), jnp.float32)
    for p in range(2 * LEVELS):
        x_rim = jnp.where(lane // 4 == p, pltpu.roll(field[p], shift + 4 * p, 1), x_rim)
    pack_rims(tile, x_rim, lambda p: field[p, :8], lambda p: field[p, S - 8 :], out)


def first_kernel(
    tracers_in,
    east_in,
    north_in,
    mixing,
    depths_in,
    neighbours_in,
    vertical_in,
    flow_out,
    rims_out,
    start_out,
    levels_out,
    tracers,
    east,
    north,
    depths,
    neighbours,
    vertical,
    block,
    arrived,
    sent,
):
    copies = [
        pltpu.make_async_copy(source, target, arrived.at[i])
        for i, (source, target) in enumerate(
            (
                (east_in, east),
                (north_in, north),
                (depths_in, depths),
                (neighbours_in, neighbours),
                (vertical_in, vertical),
                (tracers_in, tracers),
            )
        )
    ]
    for copy in copies:
        copy.start()
    for copy in copies[:2]:
        copy.wait()
    block[:S] = east[...]
    block[S : 2 * S] = north[...]
    last = jnp.broadcast_to(mixing[...].astype(jnp.float32), (16, S))
    block[2 * S :] = last.astype(jnp.bfloat16)
    leaving = [pltpu.make_async_copy(block, flow_out.at[j], sent.at[j]) for j in range(LEVELS)]
    for copy in leaving:
        copy.start()
    for copy in copies[2:]:
        copy.wait()
    tile = lax.axis_index("tile")
    depth = depths[tile]

    for k in range(LEVELS):
        wet = (k < depth).astype(jnp.float32)
        levels_out[k : k + 1] = jnp.full((1, S), wet, jnp.float32)
        levels_out[LEVELS + k : LEVELS + k + 1] = jnp.full((1, S), wet * vertical[k], jnp.float32)
    for e in range(4):
        slot = neighbours[e, tile]
        slot = jnp.where(slot < 0, -9, slot).astype(jnp.float32)
        levels_out[2 * LEVELS + e : 2 * LEVELS + e + 1] = jnp.full((1, S), slot, jnp.float32)
    for p in range(2 * LEVELS):
        start_out[p] = tracers[p] * (p % LEVELS < depth).astype(jnp.float32)
    rims(start_out, neighbours[1, tile] >= 0, tile, rims_out)
    for copy in leaving:
        copy.wait()


def ghosts(near, tile, received):
    gx, gs, gn = (jnp.zeros((S // 2, S), jnp.float32) for _ in range(3))
    mate, own, other = received
    chip = tile // 2
    for steps in (-2, -1, 1, 2):
        slot = (tile + steps).astype(jnp.float32)
        from_chip = (tile + 2 * TILES + steps) // 2 - TILES
        is_mate = from_chip == chip
        is_own = (from_chip > chip) == looks_up(tile)
        pair = jnp.minimum(from_chip, chip)
        y_at = jnp.where((tile + steps - pair) % 2 == 0, 2, 1)
        if abs(steps) == 1:
            in_row = (slot == near[0]) | (slot == near[1])
            block = jnp.where(is_own, own[0], other[0])
            block = jnp.where(is_mate, mate[0], block)
            gx = jnp.where(in_row, block.astype(jnp.float32), gx)
            mate_y = jnp.where(tile % 4 < 2, mate[2], mate[1])
            block = jnp.where(is_mate, mate_y, jnp.where(is_own, own[y_at], other[y_at]))
        else:
            block = jnp.where(is_own, own[y_at], other[y_at])
        block = block.astype(jnp.float32)
        gs = jnp.where(slot == near[2], block, gs)
        gn = jnp.where(slot == near[3], block, gn)
    return jnp.concatenate([gx, pltpu.roll(gx, S // 2, 1)], 0), gs, gn


def dot(a, b):
    return jnp.dot(a, b, preferred_element_type=jnp.float32)


def split(q):
    high = q.astype(jnp.bfloat16)
    return high, (q - high.astype(jnp.float32)).astype(jnp.bfloat16)


def inner_sums(values, right, left, emit):
    for k in range(LEVELS):
        pair = [values(k), values(k + LEVELS)]
        parts = [split(q) for q in pair]
        along_x = dot(jnp.concatenate([jnp.concatenate(q, 1) for q in parts], 0), right[...])
        along_y = dot(left[...], jnp.concatenate([jnp.concatenate(q, 0) for q in parts], 1))
        for t in range(2):
            z = second_difference(values, k + t * LEVELS)
            emit(k + t * LEVELS, along_x[t * S : (t + 1) * S], along_y[:, t * S : (t + 1) * S], z)


def second_difference(values, p):
    z = -2.0 * values(p)
    if p % LEVELS > 0:
        z = z + values(p - 1)
    if p % LEVELS < LEVELS - 1:
        z = z + values(p + 1)
    return z


def rim_changes(near, tile, received, flow, along, right_rim_packed, left_rim):
    gx, gs, gn = ghosts(near, tile, received)
    sums = dot(gx.astype(jnp.bfloat16), right_rim_packed[...])
    u = along[:S]
    change = carried(u, along[S : S + 1], sums[:, :S], sums[:, S : 2 * S], sums[:, 2 * S :])
    packed = along[S + 8 : S + 9] * change
    side_east = near[1] >= 0
    packed = jnp.where(side_east, pltpu.roll(packed, S - 8, 1), packed)
    window = jnp.where(side_east, 15, 0)
    in_window = iota((S, S), 1) // 8 == window

    def rows(p):
        return jnp.where(in_window, pltpu.roll(packed, (S - 8 * p) % S, 1), 0.0)

    sums_y = []
    for odd in range(2):
        y_rims = [
            jnp.concatenate([gs[8 * t : 8 * t + 8], gn[8 * t : 8 * t + 8]], 0)
            for t in range(LEVELS)
        ]
        sums_y.append(dot(left_rim[odd], jnp.concatenate(y_rims, 1).astype(jnp.bfloat16)))

    def ends(p):
        _, v, mixing = flow_of(flow, p % LEVELS)
        v = jnp.concatenate([v[:8], v[S - 8 :]], 0)
        y = sums_y[p % 2][:, S * (p // 2) : S * (p // 2 + 1)]
        return carried(v, mixing, y[:16], y[16:32], y[32:])

    return rows, ends


def add_ends(plane, ends):
    return jnp.concatenate(
        [plane[:8] + ends[:8], plane[8 : S - 8], plane[S - 8 :] + ends[8:]], 0
    )


def bands_kernel(
    start,
    neighbours,
    after,
    columns,
    right,
    left,
    right_rim,
    left_rim,
    right_packed,
    right_rim_packed,
    left_edge,
    left_rim_packed,
    repack,
):
    tile = lax.axis_index("tile")
    side_east = neighbours[1, tile] >= 0
    row, lane = iota((S, S), 0), iota((S, S), 1)
    own = bands(row - lane, 1)
    right[...] = jnp.concatenate([own, own], 0)
    own = bands(lane - row, 0)
    left[...] = jnp.concatenate([own, own], 1)
    base = jnp.where(side_east, S, -4)
    right_rim[...] = bands(row % 4 + base - lane, 1)
    own = bands(jnp.where(row // 8 == lane // 8, row % 8 - lane % 8, S), 1)
    right_packed[...] = jnp.concatenate([own, own], 0)
    base = jnp.where(side_east, 8, -4)
    right_rim_packed[...] = bands(
        jnp.where(row // 4 == lane // 8, row % 4 + base - lane % 8, S), 1
    )
    at = row % 8 - jnp.where(side_east, 4, 0)
    moves = (row // 8 == lane // 4) & (at == lane % 4)
    repack[...] = jnp.where(moves, 1.0, 0.0).astype(jnp.bfloat16)
    out = iota((16, 48), 0)
    out = jnp.where(out < 8, out, out + S - 16)
    column = iota((16, 48), 1)
    cell = column % 16
    same = jnp.where(cell < 8, cell, cell + S - 16)
    rim = jnp.where(cell < 8, cell % 4 - 4, cell % 4 + S)
    for odd in range(2):
        mine = jnp.where((cell // 4) % 2 == odd, rim, -2 * S)
        left_edge[odd] = bands(jnp.where(column < 32, same, mine) - out, 0)
        left_rim[odd] = bands(mine[:, :16] - out[:, :16], 0)
    cell = column[:, :16]
    both = jnp.where(cell < 4, cell - 4, jnp.where(cell < 8, cell + S - 4, -2 * S))
    left_rim_packed[...] = bands(both - out[:, :16], 0)
    packed = jnp.zeros((S, S), jnp.float32)
    shift = jnp.where(side_east, 8, 0)
    for p in range(2 * LEVELS):
        packed = jnp.where(lane // 8 == p, pltpu.roll(start[p], shift + 8 * p, 1), packed)
    columns[...] = packed


def flow_of(flow, k):
    u = flow[k, :S].astype(jnp.float32)
    v = flow[k, S : 2 * S].astype(jnp.float32)
    return u, v, flow[k, 2 * S : 2 * S + 16].astype(jnp.float32)[:1]


def inner_change(u, v, mixing, x_ahead, x_behind, y_ahead, y_behind, curve):
    carry = u * jnp.where(u >= 0, x_ahead, x_behind) + v * jnp.where(v >= 0, y_ahead, y_behind)
    return mixing * curve - carry * (1.0 / 60.0)


def carried(flow, mixing, ahead, behind, curve):
    return mixing * curve - flow * jnp.where(flow >= 0, ahead, behind) * (1.0 / 60.0)


def wet_of(levels, k):
    return levels[k : k + 1]


def lift_of(levels, k):
    return levels[LEVELS + k : LEVELS + k + 1]


def edge_kernel(
    start,
    columns,
    flow,
    levels,
    mate,
    own,
    other,
    right,
    right_rim,
    left,
    right_packed,
    right_rim_packed,
    left_edge,
    left_rim_packed,
    repack,
    rims_out,
    along_out,
):
    tile = lax.axis_index("tile")
    near = beside(levels)
    gx, gs, gn = ghosts(near, tile, (mate, own, other))
    planes = 2 * LEVELS

    side_east = near[1] >= 0
    block = iota((S, S), 1) // 8

    def gather(arrays):
        first = last = jnp.zeros(arrays[0].shape, jnp.float32)
        at = block[: first.shape[0]]
        for p, array in enumerate(arrays):
            rolled = pltpu.roll(array, 8 * p, 1) if p else array
            first = jnp.where(at == p, rolled, first)
            last = jnp.where(at == (p + 15) % 16, rolled, last)
        return jnp.where(side_east, pltpu.roll(last, 8, 1), first)

    flows = [flow_of(flow, k) for k in range(LEVELS)]
    u_packed = gather([u for u, _, _ in flows])
    v_packed = gather([v for _, v, _ in flows])
    row_block = block[:1] % LEVELS
    mixing, wet, lift = (jnp.zeros((1, S), jnp.float32) for _ in range(3))
    for k in range(LEVELS):
        mixing = jnp.where(row_block == k, flows[k][2], mixing)
        wet = jnp.where(row_block == k, wet_of(levels, k), wet)
        lift = jnp.where(row_block == k, lift_of(levels, k), lift)
    u_packed = jnp.where(block < LEVELS, u_packed, pltpu.roll(u_packed, S // 2, 1))
    v_packed = jnp.where(block < LEVELS, v_packed, pltpu.roll(v_packed, S // 2, 1))
    along_out[:S] = u_packed
    along_out[S : S + 8] = jnp.broadcast_to(mixing, (8, S))
    along_out[S + 8 :] = jnp.broadcast_to(wet, (8, S))
    low = iota((8, S), 0) < 4
    both_rims = []
    for p in range(planes):
        at = 8 * (p // 2)
        pair = (gs[at : at + 8], gn[at : at + 8])
        if p % 2:
            both_rims.append(jnp.where(low, pltpu.roll(pair[0], 4, 0), pair[1]))
        else:
            both_rims.append(jnp.where(low, pair[0], pltpu.roll(pair[1], 4, 0)))
    rim = gather(both_rims)
    rim = jnp.concatenate([rim, jnp.zeros_like(rim)], 0).astype(jnp.bfloat16)
    q = columns[...]
    parts = split(q)
    x = dot(jnp.concatenate(parts, 1), right_packed[...])
    x = x + dot(gx.astype(jnp.bfloat16), right_rim_packed[...])
    y = dot(left[...], jnp.concatenate(parts, 0))
    y_rim = dot(left_rim_packed[...], rim)
    y = [
        jnp.concatenate(
            [
                y[i * S : i * S + 8] + y_rim[16 * i : 16 * i + 8],
                y[i * S + 8 : (i + 1) * S - 8],
                y[(i + 1) * S - 8 : (i + 1) * S] + y_rim[16 * i + 8 : 16 * i + 16],
            ],
            0,
        )
        for i in range(3)
    ]
    z = -2.0 * q
    z = z + jnp.where(block % LEVELS > 0, pltpu.roll(q, 8, 1), 0.0)
    z = z + jnp.where(block % LEVELS < LEVELS - 1, pltpu.roll(q, S - 8, 1), 0.0)
    change = inner_change(
        u_packed, v_packed, mixing, x[:, :S], x[:, S : 2 * S], y[0], y[1], x[:, 2 * S :] + y[2]
    )
    section = q + (wet * change + lift * z)
    x_rim = dot(section.astype(jnp.bfloat16), repack[...])

    def ends(a):
        return jnp.concatenate([a[:8], a[S - 8 :]], 0)

    values = [jnp.concatenate([start[p, :8], start[p, S - 8 :]], 0) for p in range(planes)]
    parts = [split(q) for q in values]
    gx_ends = ends(gx)
    lane_block = iota((16, S), 1) // 4
    x_rims = [jnp.where(lane_block == p, gx_ends, 0.0) for p in range(planes)]
    x = dot(jnp.concatenate([jnp.concatenate(q, 1) for q in parts], 0), right[...])
    x = x + dot(jnp.concatenate(x_rims, 0).astype(jnp.bfloat16), right_rim[...])
    ys = []
    for odd in range(2):
        sources = []
        for p in range(odd, planes, 2):
            at = 8 * (p // 2)
            y_rims = jnp.concatenate([gs[at : at + 8], gn[at : at + 8]], 0).astype(jnp.bfloat16)
            sources.append(jnp.concatenate([*parts[p], y_rims], 0))
        ys.append(dot(left_edge[odd], jnp.concatenate(sources, 1)))
    sections = []
    for p in range(planes):
        k = p % LEVELS
        u = ends(flow[k, :S].astype(jnp.float32))
        v = ends(flow[k, S : 2 * S].astype(jnp.float32))
        m = flow[k, 2 * S : 2 * S + 16].astype(jnp.float32)
        xp = x[16 * p : 16 * p + 16]
        yp = ys[p % 2][:, S * (p // 2) : S * (p // 2 + 1)]
        change = inner_change(
            u, v, m, xp[:, :S], xp[:, S : 2 * S], yp[:16], yp[16:32], xp[:, 2 * S :] + yp[32:]
        )
        z = second_difference(lambda i: values[i], p)
        sections.append(values[p] + (wet_of(levels, k) * change + lift_of(levels, k) * z))
    pack_rims(tile, x_rim, lambda p: sections[p][:8], lambda p: sections[p][8:], rims_out)


def middle_kernel(
    start,
    flow,
    levels,
    mate,
    own,
    other,
    right,
    left,
    along,
    right_rim_packed,
    left_rim,
    after,
    out,
    section,
):
    tile = lax.axis_index("tile")
    near = beside(levels)
    received = (mate, own, other)
    rows, ends = rim_changes(near, tile, received, flow, along, right_rim_packed, left_rim)

    def inner(p, x, y, z):
        k = p % LEVELS
        u, v, mixing = flow_of(flow, k)
        curve = x[:, 2 * S :] + y[2 * S :]
        change = inner_change(
            u, v, mixing, x[:, :S], x[:, S : 2 * S], y[:S], y[S : 2 * S], curve
        )
        return wet_of(levels, k) * change + lift_of(levels, k) * z

    def first(p, x, y, z):
        plane = start[p] + (inner(p, x, y, z) + rows(p))
        section[p] = add_ends(plane, wet_of(levels, p % LEVELS) * ends(p))

    def second(p, x, y, z):
        out[p] = 0.5 * (start[p] + section[p] + inner(p, x, y, z))

    inner_sums(lambda p: start[p], right, left, first)
    inner_sums(lambda p: section[p], right, left, second)


def last_kernel(
    inner,
    flow,
    levels,
    mate,
    own,
    other,
    along,
    right_rim_packed,
    left_rim,
    out,
    held,
    sent,
):
    tile = lax.axis_index("tile")
    near = beside(levels)
    received = (mate, own, other)
    rows, ends = rim_changes(near, tile, received, flow, along, right_rim_packed, left_rim)
    copies = []
    for p in range(2 * LEVELS):
        plane = inner[p] + 0.5 * rows(p)
        held[p] = add_ends(plane, (0.5 * wet_of(levels, p % LEVELS)) * ends(p))
        copies.append(pltpu.make_async_copy(held.at[p], out.at[p], sent.at[p]))
        copies[-1].start()
    for copy in copies:
        copy.wait()


VMEM = pl.BlockSpec(memory_space=pltpu.VMEM)
SMEM = pl.BlockSpec(memory_space=pltpu.SMEM)
HBM = pl.BlockSpec(memory_space=pltpu.HBM)
ANY = pl.BlockSpec(memory_space=pl.ANY)
PARAMS = pltpu.CompilerParams(vmem_limit_bytes=24 * 1024 * 1024)
COST = pl.CostEstimate(flops=2 * 10**9, bytes_accessed=8 * 10**6, transcendentals=0)
FIELD = pltpu.VMEM((2 * LEVELS, S, S), jnp.float32)
RIMS = pltpu.VMEM((3, S // 2, S), jnp.bfloat16)


def across(mate, blocks):
    tile = lax.axis_index("tile")
    x_rim = jnp.where(tile % 4 < 2, mate[:1], blocks[:1])
    return lax.ppermute(jnp.concatenate([x_rim, mate[1:2], blocks[2:]], 0), "tile", ACROSS)


def local(
    tracers, east_velocity, north_velocity, diffusivity, vertical_diffusivity, depths, neighbours
):
    planes = 2 * LEVELS
    neighbours = neighbours.T
    inputs = (
        tracers.reshape(planes, S, S),
        east_velocity.reshape(S, S),
        north_velocity.reshape(S, S),
        diffusivity,
        depths,
        neighbours,
        vertical_diffusivity,
    )
    flow, blocks, start, levels = pl.pallas_call(
        first_kernel,
        out_shape=[
            pltpu.HBM((LEVELS, 2 * S + 16, S), jnp.bfloat16),
            RIMS,
            FIELD,
            pltpu.VMEM((3 * LEVELS, S), jnp.float32),
        ],
        in_specs=[HBM] * 3 + [VMEM] + [HBM] * 3,
        out_specs=[HBM] + [VMEM] * 3,
        scratch_shapes=[
            pltpu.VMEM((planes, S, S), jnp.float32),
            pltpu.VMEM((S, S), jnp.bfloat16),
            pltpu.VMEM((S, S), jnp.bfloat16),
            pltpu.SMEM((TILES,), jnp.int32),
            pltpu.SMEM((4, TILES), jnp.int32),
            pltpu.SMEM((LEVELS,), jnp.float32),
            pltpu.VMEM((2 * S + 16, S), jnp.bfloat16),
            pltpu.SemaphoreType.DMA((6,)),
            pltpu.SemaphoreType.DMA((LEVELS,)),
        ],
        compiler_params=PARAMS,
        name="rims",
    )(*(x if x is diffusivity else pltpu.with_memory_space_constraint(x, pltpu.HBM) for x in inputs))
    mate = lax.ppermute(blocks, "tile", MATES)
    flow = lax.all_to_all(flow, "tracer", 0, 0)
    own = across(mate, blocks)
    columns, right, left, right_rim, left_rim, *packed = pl.pallas_call(
        bands_kernel,
        out_shape=[pltpu.VMEM((S, S), jnp.float32)]
        + [
            pltpu.VMEM(shape, jnp.bfloat16)
            for shape in (
                (2 * S, 3 * S),
                (3 * S, 2 * S),
                (S, 3 * S),
                (2, 48, 16),
                (2 * S, 3 * S),
                (S, 3 * S),
                (2, 48, 48),
                (48, 16),
                (S, S),
            )
        ],
        in_specs=[VMEM, SMEM, ANY],
        out_specs=[VMEM] * 10,
        compiler_params=PARAMS,
        cost_estimate=COST,
        name="bands",
    )(start, neighbours, mate)
    own, columns = lax.optimization_barrier((own, columns))
    received = mate, own, lax.ppermute(own, "tile", MATES)
    blocks, along = pl.pallas_call(
        edge_kernel,
        out_shape=[RIMS, pltpu.VMEM((S + 16, S), jnp.float32)],
        in_specs=[VMEM] * 15,
        out_specs=[VMEM] * 2,
        compiler_params=PARAMS,
        name="edges",
    )(start, columns, flow, levels, *received, right, right_rim, left, *packed)
    mate = lax.ppermute(blocks, "tile", MATES)
    own = across(mate, blocks)
    inner = pl.pallas_call(
        middle_kernel,
        out_shape=FIELD,
        in_specs=[VMEM] * 11 + [ANY],
        out_specs=VMEM,
        scratch_shapes=[pltpu.VMEM((planes, S, S), jnp.float32)],
        compiler_params=PARAMS,
        cost_estimate=COST,
        name="middle",
    )(start, flow, levels, *received, right, left, along, packed[1], left_rim, mate)
    own, inner = lax.optimization_barrier((own, inner))
    received = mate, own, lax.ppermute(own, "tile", MATES)
    out = pl.pallas_call(
        last_kernel,
        out_shape=jax.ShapeDtypeStruct((planes, S, S), jnp.float32),
        in_specs=[VMEM] * 9,
        out_specs=HBM,
        scratch_shapes=[
            pltpu.VMEM((planes, S, S), jnp.float32),
            pltpu.SemaphoreType.DMA((planes,)),
        ],
        compiler_params=PARAMS,
        name="transported",
    )(inner, flow, levels, *received, along, packed[1], left_rim)
    return out.reshape(tracers.shape)


def solution(mesh):
    return jax.shard_map(
        local,
        mesh=mesh,
        in_specs=(
            P("tracer", "tile", None, None, None),
            P("tile", "tracer", None, None),
            P("tile", "tracer", None, None),
            P("tile", "tracer"),
            P(),
            P(),
            P(),
        ),
        out_specs=P("tracer", "tile", None, None, None),
        check_vma=False,
    )
```

```python
import jax
import jax.numpy as jnp
from jax import lax
from jax.experimental import pallas as pl
from jax.experimental.pallas import tpu as pltpu
from jax.sharding import PartitionSpec as P

S = 128
LEVELS = 8
TILES = 32
PIECES = 4
AHEAD = (-2.0, 15.0, -60.0, 20.0, 30.0, -3.0, 0.0)
BEHIND = (0.0, 3.0, -30.0, -20.0, 60.0, -15.0, 2.0)
CURVE = (0.0, 0.0, 1.0, -2.0, 1.0, 0.0, 0.0)
BANDS = (AHEAD, BEHIND, CURVE)

MATES = [(s, s ^ 1) for s in range(TILES)]
PAIRS = [(s, s + 2) for s in range(TILES - 2) if s % 4 in (0, 3)]
ACROSS = PAIRS + [(t, s) for s, t in PAIRS]


def looks_up(tile):
    return (tile % 4 == 0) | (tile % 4 == 3)


def beside(levels):
    return [levels[2 * LEVELS + e : 2 * LEVELS + e + 1] for e in range(4)]


def band(distance, coefficients):
    total = jnp.zeros(distance.shape, jnp.float32)
    for step, coefficient in zip(range(-3, 4), coefficients):
        if coefficient:
            total = jnp.where(distance == step, coefficient, total)
    return total


def iota(shape, dim):
    return lax.broadcasted_iota(jnp.int32, shape, dim)


def bands(distance, axis):
    return jnp.concatenate([band(distance, c) for c in BANDS], axis).astype(jnp.bfloat16)


def pack_rims(tile, x_rim, top, bottom, out):
    half = S // 2
    lane = iota((half, S), 1)
    x_rim = jnp.where(lane < half, x_rim[:half], pltpu.roll(x_rim[half:], half, 1))
    low = iota((8, S), 0) < 4
    south, north = [], []
    for p in range(0, 2 * LEVELS, 2):
        south.append(jnp.where(low, top(p), pltpu.roll(top(p + 1), 4, 0)))
        north.append(jnp.where(low, pltpu.roll(bottom(p), 4, 0), bottom(p + 1)))
    south, north = jnp.concatenate(south, 0), jnp.concatenate(north, 0)
    up = looks_up(tile)
    out[0] = x_rim.astype(jnp.bfloat16)
    out[1] = jnp.where(up, south, north).astype(jnp.bfloat16)
    out[2] = jnp.where(up, north, south).astype(jnp.bfloat16)


def first_kernel(
    tracers_in,
    east_in,
    north_in,
    mixing,
    depths_in,
    neighbours_in,
    vertical_in,
    flow_out,
    rims_out,
    start_out,
    levels_out,
    tracers,
    east,
    north,
    depths,
    neighbours,
    vertical,
    block,
    arrived,
    sent,
):
    planes = 2 * LEVELS
    piece = planes // PIECES
    pieces = [
        pltpu.make_async_copy(tracers_in.at[at], tracers.at[at], arrived.at[i])
        for i, at in enumerate(pl.ds(i * piece, piece) for i in range(PIECES))
    ]
    small = [
        pltpu.make_async_copy(source, target, arrived.at[PIECES + i])
        for i, (source, target) in enumerate(
            (
                (east_in, east),
                (north_in, north),
                (depths_in, depths),
                (neighbours_in, neighbours),
                (vertical_in, vertical),
            )
        )
    ]
    for copy in small[:2] + pieces + small[2:]:
        copy.start()
    for copy in small[:2]:
        copy.wait()
    block[:S] = east[...]
    block[S : 2 * S] = north[...]
    last = jnp.broadcast_to(mixing[...].astype(jnp.float32), (16, S))
    block[2 * S :] = last.astype(jnp.bfloat16)
    leaving = [pltpu.make_async_copy(block, flow_out.at[j], sent.at[j]) for j in range(LEVELS)]
    for copy in leaving:
        copy.start()
    for copy in small[2:]:
        copy.wait()
    tile = lax.axis_index("tile")
    depth = depths[tile]

    for k in range(LEVELS):
        wet = (k < depth).astype(jnp.float32)
        levels_out[k : k + 1] = jnp.full((1, S), wet, jnp.float32)
        levels_out[LEVELS + k : LEVELS + k + 1] = jnp.full((1, S), wet * vertical[k], jnp.float32)
    for e in range(4):
        slot = neighbours[e, tile]
        slot = jnp.where(slot < 0, -9, slot).astype(jnp.float32)
        levels_out[2 * LEVELS + e : 2 * LEVELS + e + 1] = jnp.full((1, S), slot, jnp.float32)
    lane = iota((S, S), 1)
    shift = jnp.where(neighbours[1, tile] >= 0, 4, 0)
    x_rim = jnp.zeros((S, S), jnp.float32)
    for p in range(planes):
        if p % piece == 0:
            pieces[p // piece].wait()
        plane = tracers[p] * (p % LEVELS < depth).astype(jnp.float32)
        start_out[p] = plane
        x_rim = jnp.where(lane // 4 == p, pltpu.roll(plane, shift + 4 * p, 1), x_rim)
    pack_rims(
        tile, x_rim, lambda p: start_out[p, :8], lambda p: start_out[p, S - 8 :], rims_out
    )
    for copy in leaving:
        copy.wait()


def ghosts(near, tile, received):
    gx, gs, gn = (jnp.zeros((S // 2, S), jnp.float32) for _ in range(3))
    mate, own, other = received
    chip = tile // 2
    for steps in (-2, -1, 1, 2):
        slot = (tile + steps).astype(jnp.float32)
        from_chip = (tile + 2 * TILES + steps) // 2 - TILES
        is_mate = from_chip == chip
        is_own = (from_chip > chip) == looks_up(tile)
        pair = jnp.minimum(from_chip, chip)
        y_at = jnp.where((tile + steps - pair) % 2 == 0, 2, 1)
        if abs(steps) == 1:
            in_row = (slot == near[0]) | (slot == near[1])
            block = jnp.where(is_own, own[0], other[0])
            block = jnp.where(is_mate, mate[0], block)
            gx = jnp.where(in_row, block.astype(jnp.float32), gx)
            mate_y = jnp.where(tile % 4 < 2, mate[2], mate[1])
            block = jnp.where(is_mate, mate_y, jnp.where(is_own, own[y_at], other[y_at]))
        else:
            block = jnp.where(is_own, own[y_at], other[y_at])
        block = block.astype(jnp.float32)
        gs = jnp.where(slot == near[2], block, gs)
        gn = jnp.where(slot == near[3], block, gn)
    return jnp.concatenate([gx, pltpu.roll(gx, S // 2, 1)], 0), gs, gn


def dot(a, b):
    return jnp.dot(a, b, preferred_element_type=jnp.float32)


def split(q):
    high = q.astype(jnp.bfloat16)
    return high, (q - high.astype(jnp.float32)).astype(jnp.bfloat16)


def inner_sums(values, right, left, emit):
    for k in range(LEVELS):
        pair = [values(k), values(k + LEVELS)]
        parts = [split(q) for q in pair]
        along_x = dot(jnp.concatenate([jnp.concatenate(q, 1) for q in parts], 0), right[...])
        along_y = dot(left[...], jnp.concatenate([jnp.concatenate(q, 0) for q in parts], 1))
        for t in range(2):
            z = second_difference(values, k + t * LEVELS)
            emit(k + t * LEVELS, along_x[t * S : (t + 1) * S], along_y[:, t * S : (t + 1) * S], z)


def second_difference(values, p):
    z = -2.0 * values(p)
    if p % LEVELS > 0:
        z = z + values(p - 1)
    if p % LEVELS < LEVELS - 1:
        z = z + values(p + 1)
    return z


def rim_changes(near, tile, received, flow, along, right_rim_packed, left_rim, scale=1.0):
    gx, gs, gn = ghosts(near, tile, received)
    sums = dot(gx.astype(jnp.bfloat16), right_rim_packed[...])
    u = along[:S]
    change = carried(u, along[S : S + 1], sums[:, :S], sums[:, S : 2 * S], sums[:, 2 * S :])
    packed = (scale * along[S + 8 : S + 9]) * change
    side_east = near[1] >= 0
    packed = jnp.where(side_east, pltpu.roll(packed, S - 8, 1), packed)
    window = jnp.where(side_east, 15, 0)
    in_window = iota((S, S), 1) // 8 == window

    def rows(p):
        return jnp.where(in_window, pltpu.roll(packed, (S - 8 * p) % S, 1), 0.0)

    sums_y = []
    for odd in range(2):
        y_rims = [
            jnp.concatenate([gs[8 * t : 8 * t + 8], gn[8 * t : 8 * t + 8]], 0)
            for t in range(LEVELS)
        ]
        sums_y.append(dot(left_rim[odd], jnp.concatenate(y_rims, 1).astype(jnp.bfloat16)))

    def ends(p):
        _, v, mixing = flow_of(flow, p % LEVELS)
        v = jnp.concatenate([v[:8], v[S - 8 :]], 0)
        y = sums_y[p % 2][:, S * (p // 2) : S * (p // 2 + 1)]
        return carried(v, mixing, y[:16], y[16:32], y[32:])

    return rows, ends


def add_ends(plane, ends):
    return jnp.concatenate(
        [plane[:8] + ends[:8], plane[8 : S - 8], plane[S - 8 :] + ends[8:]], 0
    )


def bands_kernel(
    start,
    neighbours,
    after,
    columns,
    right,
    left,
    right_rim,
    left_rim,
    right_packed,
    right_rim_packed,
    left_edge,
    left_rim_packed,
    repack,
):
    tile = lax.axis_index("tile")
    side_east = neighbours[1, tile] >= 0
    row, lane = iota((S, S), 0), iota((S, S), 1)
    own = bands(row - lane, 1)
    right[...] = jnp.concatenate([own, own], 0)
    own = bands(lane - row, 0)
    left[...] = jnp.concatenate([own, own], 1)
    base = jnp.where(side_east, S, -4)
    right_rim[...] = bands(row % 4 + base - lane, 1)
    own = bands(jnp.where(row // 8 == lane // 8, row % 8 - lane % 8, S), 1)
    right_packed[...] = jnp.concatenate([own, own], 0)
    base = jnp.where(side_east, 8, -4)
    right_rim_packed[...] = bands(
        jnp.where(row // 4 == lane // 8, row % 4 + base - lane % 8, S), 1
    )
    at = row % 8 - jnp.where(side_east, 4, 0)
    moves = (row // 8 == lane // 4) & (at == lane % 4)
    repack[...] = jnp.where(moves, 1.0, 0.0).astype(jnp.bfloat16)
    out = iota((16, 48), 0)
    out = jnp.where(out < 8, out, out + S - 16)
    column = iota((16, 48), 1)
    cell = column % 16
    same = jnp.where(cell < 8, cell, cell + S - 16)
    rim = jnp.where(cell < 8, cell % 4 - 4, cell % 4 + S)
    for odd in range(2):
        mine = jnp.where((cell // 4) % 2 == odd, rim, -2 * S)
        left_edge[odd] = bands(jnp.where(column < 32, same, mine) - out, 0)
        left_rim[odd] = bands(mine[:, :16] - out[:, :16], 0)
    cell = column[:, :16]
    both = jnp.where(cell < 4, cell - 4, jnp.where(cell < 8, cell + S - 4, -2 * S))
    left_rim_packed[...] = bands(both - out[:, :16], 0)
    packed = jnp.zeros((S, S), jnp.float32)
    shift = jnp.where(side_east, 8, 0)
    for p in range(2 * LEVELS):
        packed = jnp.where(lane // 8 == p, pltpu.roll(start[p], shift + 8 * p, 1), packed)
    columns[...] = packed


def flow_of(flow, k):
    u = flow[k, :S].astype(jnp.float32)
    v = flow[k, S : 2 * S].astype(jnp.float32)
    return u, v, flow[k, 2 * S : 2 * S + 16].astype(jnp.float32)[:1]


def inner_change(u, v, mixing, x_ahead, x_behind, y_ahead, y_behind, curve):
    carry = u * jnp.where(u >= 0, x_ahead, x_behind) + v * jnp.where(v >= 0, y_ahead, y_behind)
    return mixing * curve - carry * (1.0 / 60.0)


def carried(flow, mixing, ahead, behind, curve):
    return mixing * curve - flow * jnp.where(flow >= 0, ahead, behind) * (1.0 / 60.0)


def wet_of(levels, k):
    return levels[k : k + 1]


def lift_of(levels, k):
    return levels[LEVELS + k : LEVELS + k + 1]


def edge_kernel(
    start,
    columns,
    flow,
    levels,
    mate,
    own,
    other,
    right,
    right_rim,
    left,
    right_packed,
    right_rim_packed,
    left_edge,
    left_rim_packed,
    repack,
    rims_out,
    along_out,
):
    tile = lax.axis_index("tile")
    near = beside(levels)
    gx, gs, gn = ghosts(near, tile, (mate, own, other))
    planes = 2 * LEVELS

    side_east = near[1] >= 0
    block = iota((S, S), 1) // 8

    def gather(arrays):
        first = last = jnp.zeros(arrays[0].shape, jnp.float32)
        at = block[: first.shape[0]]
        for p, array in enumerate(arrays):
            rolled = pltpu.roll(array, 8 * p, 1) if p else array
            first = jnp.where(at == p, rolled, first)
            last = jnp.where(at == (p + 15) % 16, rolled, last)
        return jnp.where(side_east, pltpu.roll(last, 8, 1), first)

    flows = [flow_of(flow, k) for k in range(LEVELS)]
    u_packed = gather([u for u, _, _ in flows])
    v_packed = gather([v for _, v, _ in flows])
    row_block = block[:1] % LEVELS
    mixing, wet, lift = (jnp.zeros((1, S), jnp.float32) for _ in range(3))
    for k in range(LEVELS):
        mixing = jnp.where(row_block == k, flows[k][2], mixing)
        wet = jnp.where(row_block == k, wet_of(levels, k), wet)
        lift = jnp.where(row_block == k, lift_of(levels, k), lift)
    u_packed = jnp.where(block < LEVELS, u_packed, pltpu.roll(u_packed, S // 2, 1))
    v_packed = jnp.where(block < LEVELS, v_packed, pltpu.roll(v_packed, S // 2, 1))
    along_out[:S] = u_packed
    along_out[S : S + 8] = jnp.broadcast_to(mixing, (8, S))
    along_out[S + 8 :] = jnp.broadcast_to(wet, (8, S))
    low = iota((8, S), 0) < 4
    both_rims = []
    for p in range(planes):
        at = 8 * (p // 2)
        pair = (gs[at : at + 8], gn[at : at + 8])
        if p % 2:
            both_rims.append(jnp.where(low, pltpu.roll(pair[0], 4, 0), pair[1]))
        else:
            both_rims.append(jnp.where(low, pair[0], pltpu.roll(pair[1], 4, 0)))
    rim = gather(both_rims)
    rim = jnp.concatenate([rim, jnp.zeros_like(rim)], 0).astype(jnp.bfloat16)
    q = columns[...]
    parts = split(q)
    x = dot(jnp.concatenate(parts, 1), right_packed[...])
    x = x + dot(gx.astype(jnp.bfloat16), right_rim_packed[...])
    y = dot(left[...], jnp.concatenate(parts, 0))
    y_rim = dot(left_rim_packed[...], rim)
    y = [
        jnp.concatenate(
            [
                y[i * S : i * S + 8] + y_rim[16 * i : 16 * i + 8],
                y[i * S + 8 : (i + 1) * S - 8],
                y[(i + 1) * S - 8 : (i + 1) * S] + y_rim[16 * i + 8 : 16 * i + 16],
            ],
            0,
        )
        for i in range(3)
    ]
    z = -2.0 * q
    z = z + jnp.where(block % LEVELS > 0, pltpu.roll(q, 8, 1), 0.0)
    z = z + jnp.where(block % LEVELS < LEVELS - 1, pltpu.roll(q, S - 8, 1), 0.0)
    change = inner_change(
        u_packed, v_packed, mixing, x[:, :S], x[:, S : 2 * S], y[0], y[1], x[:, 2 * S :] + y[2]
    )
    section = q + (wet * change + lift * z)
    x_rim = dot(section.astype(jnp.bfloat16), repack[...])

    def ends(a):
        return jnp.concatenate([a[:8], a[S - 8 :]], 0)

    values = [jnp.concatenate([start[p, :8], start[p, S - 8 :]], 0) for p in range(planes)]
    parts = [split(q) for q in values]
    gx_ends = ends(gx)
    lane_block = iota((16, S), 1) // 4
    x_rims = [jnp.where(lane_block == p, gx_ends, 0.0) for p in range(planes)]
    x = dot(jnp.concatenate([jnp.concatenate(q, 1) for q in parts], 0), right[...])
    x = x + dot(jnp.concatenate(x_rims, 0).astype(jnp.bfloat16), right_rim[...])
    ys = []
    for odd in range(2):
        sources = []
        for p in range(odd, planes, 2):
            at = 8 * (p // 2)
            y_rims = jnp.concatenate([gs[at : at + 8], gn[at : at + 8]], 0).astype(jnp.bfloat16)
            sources.append(jnp.concatenate([*parts[p], y_rims], 0))
        ys.append(dot(left_edge[odd], jnp.concatenate(sources, 1)))
    sections = []
    for p in range(planes):
        k = p % LEVELS
        u = ends(flow[k, :S].astype(jnp.float32))
        v = ends(flow[k, S : 2 * S].astype(jnp.float32))
        m = flow[k, 2 * S : 2 * S + 16].astype(jnp.float32)
        xp = x[16 * p : 16 * p + 16]
        yp = ys[p % 2][:, S * (p // 2) : S * (p // 2 + 1)]
        change = inner_change(
            u, v, m, xp[:, :S], xp[:, S : 2 * S], yp[:16], yp[16:32], xp[:, 2 * S :] + yp[32:]
        )
        z = second_difference(lambda i: values[i], p)
        sections.append(values[p] + (wet_of(levels, k) * change + lift_of(levels, k) * z))
    pack_rims(tile, x_rim, lambda p: sections[p][:8], lambda p: sections[p][8:], rims_out)


def middle_kernel(
    start,
    flow,
    levels,
    mate,
    own,
    other,
    right,
    left,
    along,
    right_rim_packed,
    left_rim,
    after,
    out,
    section,
):
    tile = lax.axis_index("tile")
    near = beside(levels)
    received = (mate, own, other)
    rows, ends = rim_changes(near, tile, received, flow, along, right_rim_packed, left_rim)

    def inner(p, x, y, z):
        k = p % LEVELS
        u, v, mixing = flow_of(flow, k)
        curve = x[:, 2 * S :] + y[2 * S :]
        change = inner_change(
            u, v, mixing, x[:, :S], x[:, S : 2 * S], y[:S], y[S : 2 * S], curve
        )
        return wet_of(levels, k) * change + lift_of(levels, k) * z

    def first(p, x, y, z):
        plane = start[p] + (inner(p, x, y, z) + rows(p))
        section[p] = add_ends(plane, wet_of(levels, p % LEVELS) * ends(p))

    def second(p, x, y, z):
        out[p] = 0.5 * (start[p] + section[p] + inner(p, x, y, z))

    inner_sums(lambda p: start[p], right, left, first)
    inner_sums(lambda p: section[p], right, left, second)


def last_kernel(
    inner,
    flow,
    levels,
    mate,
    own,
    other,
    along,
    right_rim_packed,
    left_rim,
    out,
    held,
    sent,
):
    tile = lax.axis_index("tile")
    near = beside(levels)
    received = (mate, own, other)
    rows, ends = rim_changes(near, tile, received, flow, along, right_rim_packed, left_rim, 0.5)
    copies = []
    for p in range(2 * LEVELS):
        plane = inner[p] + rows(p)
        held[p] = add_ends(plane, (0.5 * wet_of(levels, p % LEVELS)) * ends(p))
        if p % 2:
            at = pl.ds(p - 1, 2)
            copies.append(pltpu.make_async_copy(held.at[at], out.at[at], sent.at[p]))
            copies[-1].start()
    for copy in copies:
        copy.wait()


VMEM = pl.BlockSpec(memory_space=pltpu.VMEM)
SMEM = pl.BlockSpec(memory_space=pltpu.SMEM)
HBM = pl.BlockSpec(memory_space=pltpu.HBM)
ANY = pl.BlockSpec(memory_space=pl.ANY)
PARAMS = pltpu.CompilerParams(vmem_limit_bytes=24 * 1024 * 1024)
COST = pl.CostEstimate(flops=2 * 10**9, bytes_accessed=8 * 10**6, transcendentals=0)
FIELD = pltpu.VMEM((2 * LEVELS, S, S), jnp.float32)
RIMS = pltpu.VMEM((3, S // 2, S), jnp.bfloat16)


def across(mate, blocks):
    tile = lax.axis_index("tile")
    x_rim = jnp.where(tile % 4 < 2, mate[:1], blocks[:1])
    return lax.ppermute(jnp.concatenate([x_rim, mate[1:2], blocks[2:]], 0), "tile", ACROSS)


def local(
    tracers, east_velocity, north_velocity, diffusivity, vertical_diffusivity, depths, neighbours
):
    planes = 2 * LEVELS
    neighbours = neighbours.T
    inputs = (
        tracers.reshape(planes, S, S),
        east_velocity.reshape(S, S),
        north_velocity.reshape(S, S),
        diffusivity,
        depths,
        neighbours,
        vertical_diffusivity,
    )
    flow, blocks, start, levels = pl.pallas_call(
        first_kernel,
        out_shape=[
            pltpu.HBM((LEVELS, 2 * S + 16, S), jnp.bfloat16),
            RIMS,
            FIELD,
            pltpu.VMEM((3 * LEVELS, S), jnp.float32),
        ],
        in_specs=[HBM] * 3 + [VMEM] + [HBM] * 3,
        out_specs=[HBM] + [VMEM] * 3,
        scratch_shapes=[
            pltpu.VMEM((planes, S, S), jnp.float32),
            pltpu.VMEM((S, S), jnp.bfloat16),
            pltpu.VMEM((S, S), jnp.bfloat16),
            pltpu.SMEM((TILES,), jnp.int32),
            pltpu.SMEM((4, TILES), jnp.int32),
            pltpu.SMEM((LEVELS,), jnp.float32),
            pltpu.VMEM((2 * S + 16, S), jnp.bfloat16),
            pltpu.SemaphoreType.DMA((PIECES + 5,)),
            pltpu.SemaphoreType.DMA((LEVELS,)),
        ],
        compiler_params=PARAMS,
        name="rims",
    )(*(x if x is diffusivity else pltpu.with_memory_space_constraint(x, pltpu.HBM) for x in inputs))
    mate = lax.ppermute(blocks, "tile", MATES)
    flow = lax.all_to_all(flow, "tracer", 0, 0)
    own = across(mate, blocks)
    columns, right, left, right_rim, left_rim, *packed = pl.pallas_call(
        bands_kernel,
        out_shape=[pltpu.VMEM((S, S), jnp.float32)]
        + [
            pltpu.VMEM(shape, jnp.bfloat16)
            for shape in (
                (2 * S, 3 * S),
                (3 * S, 2 * S),
                (S, 3 * S),
                (2, 48, 16),
                (2 * S, 3 * S),
                (S, 3 * S),
                (2, 48, 48),
                (48, 16),
                (S, S),
            )
        ],
        in_specs=[VMEM, SMEM, ANY],
        out_specs=[VMEM] * 10,
        compiler_params=PARAMS,
        cost_estimate=COST,
        name="bands",
    )(start, neighbours, mate)
    own, columns = lax.optimization_barrier((own, columns))
    received = mate, own, lax.ppermute(own, "tile", MATES)
    blocks, along = pl.pallas_call(
        edge_kernel,
        out_shape=[RIMS, pltpu.VMEM((S + 16, S), jnp.float32)],
        in_specs=[VMEM] * 15,
        out_specs=[VMEM] * 2,
        compiler_params=PARAMS,
        name="edges",
    )(start, columns, flow, levels, *received, right, right_rim, left, *packed)
    mate = lax.ppermute(blocks, "tile", MATES)
    own = across(mate, blocks)
    inner = pl.pallas_call(
        middle_kernel,
        out_shape=FIELD,
        in_specs=[VMEM] * 11 + [ANY],
        out_specs=VMEM,
        scratch_shapes=[pltpu.VMEM((planes, S, S), jnp.float32)],
        compiler_params=PARAMS,
        cost_estimate=COST,
        name="middle",
    )(start, flow, levels, *received, right, left, along, packed[1], left_rim, mate)
    own, inner = lax.optimization_barrier((own, inner))
    received = mate, own, lax.ppermute(own, "tile", MATES)
    out = pl.pallas_call(
        last_kernel,
        out_shape=jax.ShapeDtypeStruct((planes, S, S), jnp.float32),
        in_specs=[VMEM] * 9,
        out_specs=HBM,
        scratch_shapes=[
            pltpu.VMEM((planes, S, S), jnp.float32),
            pltpu.SemaphoreType.DMA((planes,)),
        ],
        compiler_params=PARAMS,
        name="transported",
    )(inner, flow, levels, *received, along, packed[1], left_rim)
    return out.reshape(tracers.shape)


def solution(mesh):
    return jax.shard_map(
        local,
        mesh=mesh,
        in_specs=(
            P("tracer", "tile", None, None, None),
            P("tile", "tracer", None, None),
            P("tile", "tracer", None, None),
            P("tile", "tracer"),
            P(),
            P(),
            P(),
        ),
        out_specs=P("tracer", "tile", None, None, None),
        check_vma=False,
    )
```
